32 devices in a mesh: fsdp: 4 (over z), dp: 8 (over y, x, core).
Axes of the slice: x: 2, y: 2, z: 4, core: 2. Of those that a mesh axis runs over, the one named last changes fastest.
Arguments:
- tokens: bfloat16 [8, 1536, 896], P('dp', 'fsdp'), may hold values from -6 to 6
- cotangent: bfloat16 [8, 1536, 896], P('dp', 'fsdp'), may hold values from -6 to 6
- counts: int32 [8, 4], P('dp'), may hold values from 192 to 384, as said below
- lengths: int32 [8, 3], P('dp'), may hold values from 1 to 1056, as said below
- attn_gain: bfloat16 [896], P('dp'), may hold values from 0.5 to 1.5
- w_query: bfloat16 [896, 896], P('fsdp', 'dp'), may hold values from -0.1875 to 0.1875
- b_query: bfloat16 [896], P('dp'), may hold values from -3 to 3
- w_key: bfloat16 [896, 128], P('fsdp', 'dp'), may hold values from -0.1875 to 0.1875
- w_value: bfloat16 [896, 128], P('fsdp', 'dp'), may hold values from -0.1875 to 0.1875
- b_value: bfloat16 [128], P('dp'), may hold values from -3 to 3
- w_out: bfloat16 [896, 896], P('fsdp', 'dp'), may hold values from -0.5 to 0.5
- mlp_gain: bfloat16 [896], P('dp'), may hold values from 0.5 to 1.5
- w_gate: bfloat16 [896, 4864], P('fsdp', 'dp'), may hold values from -0.1875 to 0.1875
- w_up: bfloat16 [896, 4864], P('fsdp', 'dp'), may hold values from -0.1875 to 0.1875
- w_down: bfloat16 [4864, 896], P('fsdp', 'dp'), may hold values from -0.15625 to 0.15625
Outputs:
- mixed: bfloat16 [8, 1536, 896], P('dp', 'fsdp')
- d_tokens: bfloat16 [8, 1536, 896], P('dp', 'fsdp')
- grad_attn_gain: float32 [896], P('dp')
- grad_w_query: float32 [896, 896], P('fsdp', 'dp')
- grad_b_query: float32 [896], P('dp')
- grad_w_key: float32 [896, 128], P('fsdp', 'dp')
- grad_w_value: float32 [896, 128], P('fsdp', 'dp')
- grad_b_value: float32 [128], P('dp')
- grad_w_out: float32 [896, 896], P('fsdp', 'dp')
- grad_mlp_gain: float32 [896], P('dp')
- grad_w_gate: float32 [896, 4864], P('fsdp', 'dp')
- grad_w_up: float32 [896, 4864], P('fsdp', 'dp')
- grad_w_down: float32 [4864, 896], P('fsdp', 'dp')
The draws below stay inside these ranges and needn't reach their ends.
Inputs may be any that keep to these rules, and one draw needn't show every extreme that they name: In each group the counts sum to 1152, and one count of each group equals 384. In each group the lengths sum to the group's used slots; the sequences fill the used slots of the devices in order; one sequence of each group has exactly the largest length and has tokens on the first and on the last device of fsdp.
All inputs are finite; a program needn't handle non-finite values.
Results may differ from the reference program's by a relative error of at most 0.02.
Values may be sent and summed in bfloat16 or wider, within the bound.
No kernel may reach another device: no remote copies, remote signals or barrier semaphores. Data moves between devices by JAX's collectives and lax.ppermute only.
A program may use at most 192 MiB of HBM per device.

```python
import jax
import jax.numpy as jnp
from jax import lax

D = 896
QUERY_HEADS = 14
KEY_VALUE_HEADS = 2
HEAD_SIZE = 64
FF = 4864
TOK_DEV = 384
NSEQ = 3
QW = 896
KVW = 128
GROUPS = 8
GROUP_TOK = 1536
N_FSDP = 4


def group_layout(key):
    key_rows = jax.random.split(key, 7)
    half = TOK_DEV // 2
    owners = jnp.arange(N_FSDP, dtype=jnp.int32)
    full_block = jax.random.randint(key_rows[0], (), 0, N_FSDP)
    others = owners != full_block
    weights = jnp.where(others, jax.random.randint(key_rows[1], (N_FSDP,), 4, 9), 0)
    spare = (N_FSDP - 2) * TOK_DEV // 4
    share = spare * weights // jnp.sum(weights)
    left = spare - jnp.sum(share)
    rank = jnp.cumsum(others.astype(jnp.int32)) - 1
    extra = jnp.where(others & (rank < left), 1, 0)
    counts = half + share + extra + jnp.where(others, 0, half)
    lead = jax.random.randint(key_rows[2], (), 0, NSEQ)
    trail = NSEQ - 1 - lead
    sides = TOK_DEV // 4
    before = jax.random.randint(key_rows[3], (), lead, sides - trail + 1)
    after = sides - before
    numbers = jnp.arange(NSEQ, dtype=jnp.int32)
    is_pre = numbers < lead
    is_post = numbers > lead
    pre_weight = jnp.where(is_pre, jax.random.randint(key_rows[5], (NSEQ,), 1, 9), 0)
    post_weight = jnp.where(is_post, jax.random.randint(key_rows[6], (NSEQ,), 1, 9), 0)
    pre_len = jnp.where(is_pre, 1 + (before - lead) * pre_weight // jnp.maximum(jnp.sum(pre_weight), 1), 0)
    pre_len = pre_len + jnp.where(is_pre & (numbers == 0), before - jnp.sum(pre_len), 0)
    post_len = jnp.where(is_post, 1 + (after - trail) * post_weight // jnp.maximum(jnp.sum(post_weight), 1), 0)
    post_len = post_len + jnp.where(is_post & (numbers == lead + 1), after - jnp.sum(post_len), 0)
    longest = 3 * N_FSDP * TOK_DEV // 4 - sides
    lengths = pre_len + post_len + jnp.where(numbers == lead, longest, 0)
    return (counts.astype(jnp.int32), lengths.astype(jnp.int32))


def all_layouts(key):
    return jax.vmap(group_layout)(jax.random.split(key, GROUPS))


def draw_counts(key, part):
    layout = all_layouts(key)
    return layout[0]


def draw_lengths(key, part):
    layout = all_layouts(key)
    return layout[1]


def levels(own_key, extent, cuts, low, top_value):
    factor_of = 1.0
    for dim, shards_of in cuts:
        draws = jax.random.uniform(jax.random.fold_in(jax.random.fold_in(own_key, 6), dim), (shards_of,), jnp.float32, low / len(cuts), top_value / len(cuts))
        factor_of = factor_of * jnp.repeat(jnp.exp(draws), extent[dim] // shards_of).reshape((-1,) + (1,) * (len(extent) - 1 - dim))
    return factor_of


def centred(rng, dims, spread, most, cuts=(), kind=jnp.bfloat16):
    values = jax.random.normal(rng, dims, jnp.float32) * spread
    if len(cuts) > 0:
        values = levels(rng, dims, cuts, -0.22, 0.18) * values
    return jnp.clip(values, min=-most, max=most).astype(kind)


def setup_inputs(seed: int = 0) -> dict:
    splits = jax.random.split(jax.random.key(seed), 16)
    tokens = centred(splits[0], (GROUPS, GROUP_TOK, D), 1.0, 6.0, ((0, 8), (1, 4)))
    cotangent = centred(splits[1], (GROUPS, GROUP_TOK, D), 1.0, 6.0, ((0, 8), (1, 4)))
    counts = draw_counts(jax.random.fold_in(splits[15], 71), 0)
    lengths = draw_lengths(jax.random.fold_in(splits[15], 71), 0)
    attn_gain = jnp.clip(1.0 + 0.1 * jax.random.normal(splits[4], (D,), jnp.float32), 0.5, 1.5).astype(jnp.bfloat16)
    w_query = centred(splits[5], (D, QW), D ** -0.5, 0.1875, ((0, 4), (1, 8)))
    b_query = centred(splits[6], (QW,), 0.5, 3.0, ((0, 8),))
    w_key = centred(splits[7], (D, KVW), D ** -0.5, 0.1875, ((0, 4), (1, 8)))
    w_value = centred(splits[8], (D, KVW), D ** -0.5, 0.1875, ((0, 4), (1, 8)))
    b_value = centred(splits[9], (KVW,), 0.5, 3.0, ((0, 8),))
    w_out = centred(splits[10], (QW, D), (QW // 8) ** -0.5, 0.5, ((0, 4), (1, 8)))
    mlp_gain = jnp.clip(1.0 + 0.1 * jax.random.normal(splits[11], (D,), jnp.float32), 0.5, 1.5).astype(jnp.bfloat16)
    w_gate = centred(splits[12], (D, FF), D ** -0.5, 0.1875, ((0, 4), (1, 8)))
    w_up = centred(splits[13], (D, FF), D ** -0.5, 0.1875, ((0, 4), (1, 8)))
    w_down = centred(splits[14], (FF, D), (FF // 4) ** -0.5, 0.15625, ((0, 4), (1, 8)))
    return dict(tokens=tokens, cotangent=cotangent, counts=counts, lengths=lengths, attn_gain=attn_gain, w_query=w_query, b_query=b_query, w_key=w_key, w_value=w_value, b_value=b_value, w_out=w_out, mlp_gain=mlp_gain, w_gate=w_gate, w_up=w_up, w_down=w_down)


EPS = 1e-06
THETA = 1000000.0
NEGATIVE_FILL = -1e+30

@jax.custom_vjp
def low(v):
    return lax.optimization_barrier(v.astype(jnp.bfloat16)).astype(jnp.float32)

@jax.custom_vjp
def low_back(v):
    return v

def low_keep(v):
    return (low(v), None)

def low_pass(kept, grad):
    return (grad,)

def back_keep(v):
    return (v, None)

def back_low(kept, grad):
    return (low(grad),)
low.defvjp(low_keep, low_pass)
low_back.defvjp(back_keep, back_low)

def token_meta(count_row, length_row, slot, per_device):
    device = slot // per_device
    inner = slot % per_device
    owners = jnp.arange(count_row.shape[0], dtype=jnp.int32)
    pick = (device[:, None] == owners[None, :]).astype(jnp.int32)
    before = jnp.cumsum(count_row) - count_row
    count_here = lax.optimization_barrier(jnp.sum(pick * count_row[None, :], 1))
    offset = lax.optimization_barrier(jnp.sum(pick * before[None, :], 1))
    valid_mask = inner < count_here
    block_index = offset + inner
    ends = jnp.cumsum(length_row)
    sequence_ids = lax.optimization_barrier(jnp.sum((block_index[:, None] >= ends[None, :]).astype(jnp.int32), 1))
    starts = ends - length_row
    numbers = jnp.arange(length_row.shape[0], dtype=jnp.int32)
    start_of = lax.optimization_barrier(jnp.sum((sequence_ids[:, None] == numbers[None, :]).astype(jnp.int32) * starts[None, :], 1))
    position = jnp.where(valid_mask, block_index - start_of, 0)
    sequence_ids = jnp.where(valid_mask, sequence_ids, -1)
    return (valid_mask, block_index, sequence_ids, position)

def allowed_pairs(query_meta, key_meta):
    q_valid, q_index, q_seq, q_slot = query_meta
    k_valid, k_index, k_seq, k_slot = key_meta
    same = (q_seq[:, None] == k_seq[None, :]) & q_valid[:, None] & k_valid[None, :]
    same = same & (k_index[None, :] <= q_index[:, None])
    return same | (q_slot[:, None] == k_slot[None, :])

def rope_tables(position, half):
    steps = jnp.arange(half, dtype=jnp.float32) * (1.0 / half)
    freq = THETA ** (-steps)
    angle = position[:, None] * freq[None, :]
    cosine_table = jnp.cos(angle)
    sine_table = jnp.sin(angle)
    return (jnp.concatenate([cosine_table, cosine_table], 1), jnp.concatenate([sine_table, sine_table], 1))

def rotary_apply(tensor, cosine_table, sine_table):
    half = tensor.shape[-1] // 2
    turned = jnp.concatenate([-tensor[..., half:], tensor[..., :half]], -1)
    shape = (tensor.shape[0],) + (1,) * (tensor.ndim - 2) + (tensor.shape[-1],)
    return tensor * cosine_table.reshape(shape) + turned * sine_table.reshape(shape)

def block_forward(inputs, weights, meta):
    attn_gain, w_query, b_query, w_key, w_value, b_value, w_out, mlp_gain, w_gate, w_up, w_down = weights
    valid_mask, block_index, sequence_ids, position, token_slots = meta
    highest = lax.Precision.HIGHEST
    token_count = inputs.shape[0]
    head_groups = QUERY_HEADS // KEY_VALUE_HEADS
    scale = float(HEAD_SIZE) ** (-0.5)
    valid_col = valid_mask.astype(jnp.float32)[:, None]
    inv_one = lax.rsqrt(lax.optimization_barrier(jnp.mean(inputs * inputs, -1, keepdims=True)) + EPS)
    normed = low(inputs * inv_one * attn_gain)
    query_unrotated = low_back(jnp.dot(normed, w_query, precision=highest) + b_query)
    key_unrotated = low_back(jnp.dot(normed, w_key, precision=highest))
    value_projected = low_back(jnp.dot(normed, w_value, precision=highest) + b_value)
    cosine_table, sine_table = rope_tables(position.astype(jnp.float32), HEAD_SIZE // 2)
    query_rows = low(rotary_apply(query_unrotated.reshape(token_count, KEY_VALUE_HEADS, head_groups, HEAD_SIZE), cosine_table, sine_table))
    key_rows = low(rotary_apply(key_unrotated.reshape(token_count, KEY_VALUE_HEADS, HEAD_SIZE), cosine_table, sine_table))
    value_rows = low(value_projected.reshape(token_count, KEY_VALUE_HEADS, HEAD_SIZE))
    block_step = min(512, token_count)
    block_count = token_count // block_step

    def attend_forward(args):
        query_blk, valid_blk, index_blk, seq_blk, slot_blk = args
        raw = jnp.einsum('qgjd,kgd->gjqk', query_blk, key_rows, precision=highest) * scale
        raw = low_back(raw)
        allowed = allowed_pairs((valid_blk, index_blk, seq_blk, slot_blk), (valid_mask, block_index, sequence_ids, token_slots))
        masked = jnp.where(allowed[None, None], raw, NEGATIVE_FILL)
        top = lax.optimization_barrier(jnp.max(masked, -1, keepdims=True))
        log_total = top + jnp.log(lax.optimization_barrier(jnp.sum(jnp.exp(masked - top), -1, keepdims=True)))
        probs = low(jnp.exp(masked - log_total))
        return jnp.einsum('gjqk,kgd->qgjd', probs, value_rows, precision=highest)
    attention_output = lax.map(jax.checkpoint(attend_forward), (query_rows.reshape(block_count, block_step, KEY_VALUE_HEADS, head_groups, HEAD_SIZE), valid_mask.reshape(block_count, block_step), block_index.reshape(block_count, block_step), sequence_ids.reshape(block_count, block_step), token_slots.reshape(block_count, block_step)))
    attention_output = attention_output.reshape(token_count, QUERY_HEADS * HEAD_SIZE)
    heads_out = low_back(low(attention_output))
    proj = low_back(jnp.dot(heads_out, w_out, precision=highest))
    hidden = inputs + valid_col * proj
    inv_two = lax.rsqrt(lax.optimization_barrier(jnp.mean(hidden * hidden, -1, keepdims=True)) + EPS)
    normed2 = low(hidden * inv_two * mlp_gain)
    gate = low_back(jnp.dot(normed2, w_gate, precision=highest))
    up_val = low_back(jnp.dot(normed2, w_up, precision=highest))
    act = low(jax.nn.silu(gate) * up_val)
    down = low_back(jnp.dot(act, w_down, precision=highest))
    return hidden + valid_col * down

def reference(tokens, cotangent, counts, lengths, attn_gain, w_query, b_query, w_key, w_value, b_value, w_out, mlp_gain, w_gate, w_up, w_down):
    params = tuple((p.astype(jnp.float32) for p in (attn_gain, w_query, b_query, w_key, w_value, b_value, w_out, mlp_gain, w_gate, w_up, w_down)))
    token_slots = jnp.arange(GROUP_TOK, dtype=jnp.int32)

    def one_group(totals, inputs):
        block_in, block_cot, count_row, length_row = inputs
        valid_mask, block_index, sequence_ids, position = token_meta(count_row, length_row, token_slots, TOK_DEV)
        meta = (valid_mask, block_index, sequence_ids, position, token_slots)

        def forward(values_in, *weights):
            return block_forward(values_in, weights, meta)
        result, pull = jax.vjp(forward, block_in.astype(jnp.float32), *params)
        grads = pull(block_cot.astype(jnp.float32))
        totals = tuple((t + g for t, g in zip(totals, grads[1:])))
        return (totals, (result.astype(jnp.bfloat16), grads[0].astype(jnp.bfloat16)))
    zero_fill = tuple((jnp.zeros(p.shape, jnp.float32) for p in params))
    totals, (mixed, d_tokens) = lax.scan(one_group, zero_fill, (tokens, cotangent, counts, lengths))
    return (mixed, d_tokens, totals[0], totals[1], totals[2], totals[3], totals[4], totals[5], totals[6], totals[7], totals[8], totals[9], totals[10])
```

```python
import jax
import jax.numpy as jnp
from jax import lax
from jax.sharding import PartitionSpec as P

QUERY_HEADS = 14
KEY_VALUE_HEADS = 2
HEAD_SIZE = 64


EPS = 1e-06
THETA = 1000000.0
NEGATIVE_FILL = -1e30


def shortened(array):
    return jax.tree.map(lambda a: a.astype(jnp.bfloat16) if a.dtype == jnp.float32 else a, array)


def token_meta(count_row, length_row, slot, per_device):
    device = slot // per_device
    inner = slot % per_device
    owners = jnp.arange(count_row.shape[0], dtype=jnp.int32)
    pick = (device[:, None] == owners[None, :]).astype(jnp.int32)
    before = jnp.cumsum(count_row) - count_row
    count_here = jnp.sum(pick * count_row[None, :], 1)
    offset = jnp.sum(pick * before[None, :], 1)
    valid_mask = inner < count_here
    block_index = offset + inner
    ends = jnp.cumsum(length_row)
    sequence_ids = jnp.sum((block_index[:, None] >= ends[None, :]).astype(jnp.int32), 1)
    starts = ends - length_row
    numbers = jnp.arange(length_row.shape[0], dtype=jnp.int32)
    start_of = jnp.sum(
        (sequence_ids[:, None] == numbers[None, :]).astype(jnp.int32) * starts[None, :], 1
    )
    position = jnp.where(valid_mask, block_index - start_of, 0)
    sequence_ids = jnp.where(valid_mask, sequence_ids, -1)
    return (valid_mask, block_index, sequence_ids, position)


def allowed_pairs(query_meta, key_meta):
    q_valid, q_index, q_seq, q_slot = query_meta
    k_valid, k_index, k_seq, k_slot = key_meta
    same = (q_seq[:, None] == k_seq[None, :]) & q_valid[:, None] & k_valid[None, :]
    same = same & (k_index[None, :] <= q_index[:, None])
    return same | (q_slot[:, None] == k_slot[None, :])


def rope_tables(position, half):
    steps = jnp.arange(half, dtype=jnp.float32) * (1.0 / half)
    freq = THETA ** (-steps)
    angle = position[:, None] * freq[None, :]
    cosine_table = jnp.cos(angle)
    sine_table = jnp.sin(angle)
    return (
        jnp.concatenate([cosine_table, cosine_table], 1),
        jnp.concatenate([sine_table, sine_table], 1),
    )


def table_shape(tensor):
    return (tensor.shape[0],) + (1,) * (tensor.ndim - 2) + (tensor.shape[-1],)


def rotary_apply(tensor, cosine_table, sine_table):
    half = tensor.shape[-1] // 2
    turned = jnp.concatenate([-tensor[..., half:], tensor[..., :half]], -1)
    shape = table_shape(tensor)
    return tensor * cosine_table.reshape(shape) + turned * sine_table.reshape(shape)


def rotary_reverse(tensor, cosine_table, sine_table):
    half = tensor.shape[-1] // 2
    shape = table_shape(tensor)
    moved = tensor * sine_table.reshape(shape)
    turned = jnp.concatenate([moved[..., half:], -moved[..., :half]], -1)
    return tensor * cosine_table.reshape(shape) + turned


def flip(array, mask, size):
    return lax.ppermute(array, "dp", [(i, i ^ mask) for i in range(size)])


def gather_tokens(rows, size):
    if size != 8:
        return lax.all_gather(rows, "dp", axis=0)
    half = rows.shape[0] // 2
    by_x, by_y, by_core = flip(rows, 2, 8), flip(rows, 4, 8), flip(rows, 1, 8)
    far_a, far_b = flip(by_x[:half], 4, 8), flip(by_y[half:], 2, 8)
    core_x, core_y = flip(by_x, 1, 8), flip(by_y, 1, 8)
    core_a, core_b = flip(far_a, 1, 8), flip(far_b, 1, 8)
    return jnp.stack(
        [
            rows,
            by_core,
            by_x,
            core_x,
            by_y,
            core_y,
            jnp.concatenate([far_a, far_b]),
            jnp.concatenate([core_a, core_b]),
        ]
    )


def scatter_tokens(parts, size):
    if size != 8:
        return lax.psum_scatter(
            parts.astype(jnp.bfloat16), "dp", scatter_dimension=0, tiled=False
        ).astype(jnp.float32)
    sent = parts.astype(jnp.bfloat16)
    half = parts.shape[1] // 2
    wide = jnp.float32
    seven, five, three, one = [flip(sent[k], 1, 8) for k in (7, 5, 3, 1)]
    far = (parts[6].astype(wide) + seven.astype(wide)).astype(jnp.bfloat16)
    far_x, far_y = flip(far[:half], 2, 8), flip(far[half:], 4, 8)
    on_y = parts[4].astype(wide) + five.astype(wide)
    on_x = parts[2].astype(wide) + three.astype(wide)
    on_y = jnp.concatenate([on_y[:half] + far_x.astype(wide), on_y[half:]]).astype(jnp.bfloat16)
    on_x = jnp.concatenate([on_x[:half], on_x[half:] + far_y.astype(wide)]).astype(jnp.bfloat16)
    got_x, got_y = flip(on_x, 2, 8), flip(on_y, 4, 8)
    own = parts[0].astype(wide) + one.astype(wide)
    return own + got_x.astype(wide) + got_y.astype(wide)


def exchange(parts, size):
    if size != 8:
        return lax.all_to_all(parts, "dp", 0, 0, tiled=True)
    place = lax.axis_index("dp")
    result = parts
    for k in range(1, 8):
        piece = flip(lax.dynamic_index_in_dim(parts, place ^ k, 0, True), k, 8)
        result = lax.dynamic_update_slice_in_dim(result, piece, place ^ k, 0)
    return result


def gather_rows(rows, size):
    place = lax.axis_index("fsdp")
    result = jnp.zeros((size,) + rows.shape, rows.dtype)
    result = lax.dynamic_update_slice_in_dim(result, rows[None], place, 0)
    for k in range(1, size):
        piece = lax.ppermute(rows, "fsdp", [(i, (i + k) % size) for i in range(size)])
        result = lax.dynamic_update_slice_in_dim(result, piece[None], (place + size - k) % size, 0)
    return result


def scatter_rows(parts, size):
    place = lax.axis_index("fsdp")
    sent = parts.astype(jnp.bfloat16)
    total = lax.dynamic_index_in_dim(parts, place, 0, False).astype(jnp.float32)
    for k in range(1, size):
        piece = lax.dynamic_index_in_dim(sent, (place + k) % size, 0, False)
        total = total + lax.ppermute(
            piece, "fsdp", [(i, (i + k) % size) for i in range(size)]
        ).astype(jnp.float32)
    return total


def dot_tn(left, right):
    return lax.dot_general(
        left, right, (((0,), (0,)), ((), ())), preferred_element_type=jnp.float32
    )


def dot_nt(left, right):
    return lax.dot_general(
        left, right, (((1,), (1,)), ((), ())), preferred_element_type=jnp.float32
    )


def dot_nn(left, right):
    return jnp.dot(left, right, preferred_element_type=jnp.float32)


def body(
    tokens,
    cotangent,
    counts,
    lengths,
    attn_gain,
    w_query,
    b_query,
    w_key,
    w_value,
    b_value,
    w_out,
    mlp_gain,
    w_gate,
    w_up,
    w_down,
):
    lanes = lax.axis_size("dp")
    fsdp_place = lax.axis_index("fsdp")
    token_rows = tokens.shape[1]
    grouped_rows = token_rows * lax.axis_size("fsdp")
    head_groups = QUERY_HEADS // KEY_VALUE_HEADS
    scale = float(HEAD_SIZE) ** (-0.5)
    inputs = tokens[0].astype(jnp.float32)
    group_slots = jnp.arange(grouped_rows, dtype=jnp.int32)
    k_valid, k_index, k_seq, k_pos = token_meta(counts[0], lengths[0], group_slots, token_rows)
    own_start = fsdp_place * token_rows
    q_valid = lax.dynamic_slice_in_dim(k_valid, own_start, token_rows)
    q_index = lax.dynamic_slice_in_dim(k_index, own_start, token_rows)
    q_seq = lax.dynamic_slice_in_dim(k_seq, own_start, token_rows)
    q_pos = lax.dynamic_slice_in_dim(k_pos, own_start, token_rows)
    q_slot = lax.dynamic_slice_in_dim(group_slots, own_start, token_rows)
    query_meta = (q_valid, q_index, q_seq, q_slot)
    valid_col = q_valid.astype(jnp.float32)[:, None]
    fsdp_size = lax.axis_size("fsdp")
    width = tokens.shape[2]
    query_part, key_part, out_part = w_query.shape[1], w_key.shape[1], w_out.shape[1]
    hidden_part = w_gate.shape[1]
    pieces_each = lanes // fsdp_size
    vector_widths = (query_part, query_part, key_part, query_part)
    projections = lax.all_gather(
        jnp.concatenate([w_query, w_key, w_value, w_out], 1), "fsdp", axis=0, tiled=True
    ).T
    joint_rows = projections.shape[0]
    vector_row = jnp.concatenate([attn_gain, b_query, b_value, mlp_gain])
    vector_count = vector_row.shape[0]
    vector_block = jnp.zeros((16, width), jnp.bfloat16).at[0, :vector_count].set(vector_row)
    spread = lax.all_gather(jnp.concatenate([projections, vector_block]), "dp", axis=0)
    edges = (0, query_part, query_part + key_part, query_part + 2 * key_part, joint_rows)
    wq_t, wk_t, wv_t, wo_t = [
        spread[:, edges[i] : edges[i + 1]].reshape(-1, width) for i in range(4)
    ]
    joint_t = jnp.concatenate([wq_t, wk_t, wv_t])
    vector_table = spread[:, joint_rows, :vector_count].astype(jnp.float32)
    marks = [0]
    for size in vector_widths:
        marks.append(marks[-1] + size)
    gain_one, query_bias_vector, bias_value, gain_two = [
        vector_table[:, marks[i] : marks[i + 1]].reshape(-1) for i in range(4)
    ]
    down_t = w_down.T.reshape(out_part, pieces_each, hidden_part).transpose(1, 0, 2)
    hidden_slabs = lax.all_gather(
        jnp.concatenate([w_gate, w_up, down_t.reshape(-1, hidden_part)]), "fsdp", axis=0
    )
    rows_each = w_gate.shape[0]
    gate_w = hidden_slabs[:, :rows_each].reshape(width, hidden_part)
    up_w = hidden_slabs[:, rows_each : 2 * rows_each].reshape(width, hidden_part)
    down_w = exchange(
        hidden_slabs[:, 2 * rows_each :].reshape(lanes, out_part, hidden_part), lanes
    ).reshape(width, hidden_part)
    grad_out = cotangent[0].astype(jnp.float32)
    d_down = (valid_col * grad_out).astype(jnp.bfloat16)
    d_down_all = gather_tokens(d_down, lanes).reshape(-1, width)
    inv_one = lax.rsqrt(jnp.mean(inputs * inputs, -1, keepdims=True) + EPS)
    unit_one = inputs * inv_one
    normed = (unit_one * gain_one).astype(jnp.bfloat16)
    joint = dot_nt(normed, joint_t)
    query_width, key_width = QUERY_HEADS * HEAD_SIZE, KEY_VALUE_HEADS * HEAD_SIZE
    query_portion = joint[:, :query_width]
    key_portion = joint[:, query_width : query_width + key_width]
    v_part = joint[:, query_width + key_width :]
    cosine_table, sine_table = rope_tables(q_pos.astype(jnp.float32), HEAD_SIZE // 2)
    query_heads = rotary_apply(
        (query_portion + query_bias_vector).reshape(
            token_rows, KEY_VALUE_HEADS, head_groups, HEAD_SIZE
        ),
        cosine_table,
        sine_table,
    ).astype(jnp.bfloat16)
    key_head_rows = rotary_apply(
        key_portion.reshape(token_rows, KEY_VALUE_HEADS, HEAD_SIZE), cosine_table, sine_table
    ).astype(jnp.bfloat16)
    value_heads = (v_part + bias_value).astype(jnp.bfloat16)
    gathered = gather_rows(
        jnp.concatenate(
            [key_head_rows.reshape(token_rows, KEY_VALUE_HEADS * HEAD_SIZE), value_heads], 1
        ),
        fsdp_size,
    ).reshape(grouped_rows, 2 * KEY_VALUE_HEADS * HEAD_SIZE)
    gathered_keys = gathered[:, : KEY_VALUE_HEADS * HEAD_SIZE]
    gathered_values = gathered[:, KEY_VALUE_HEADS * HEAD_SIZE :]
    key_block_slice = min(512, grouped_rows)
    block_count = grouped_rows // key_block_slice
    block_tiles = (
        gathered_keys.reshape(block_count, key_block_slice, KEY_VALUE_HEADS, HEAD_SIZE),
        gathered_values.reshape(block_count, key_block_slice, KEY_VALUE_HEADS, HEAD_SIZE),
        k_valid.reshape(block_count, key_block_slice),
        k_index.reshape(block_count, key_block_slice),
        k_seq.reshape(block_count, key_block_slice),
        group_slots.reshape(block_count, key_block_slice),
    )

    def scores(tile):
        raw = (
            jnp.einsum("qgjd,kgd->gjqk", query_heads, tile[0], preferred_element_type=jnp.float32)
            * scale
        )
        allowed = allowed_pairs(query_meta, (tile[2], tile[3], tile[4], tile[5]))
        return (jnp.where(allowed[None, None], raw, NEGATIVE_FILL), allowed)

    def stats(carry, tile):
        top, total = carry
        masked, allowed = scores(tile)
        new_top = jnp.maximum(top, jnp.max(masked, -1))
        shifted = jnp.where(allowed[None, None], jnp.exp(masked - new_top[..., None]), 0.0)
        total = total * jnp.exp(top - new_top) + jnp.sum(shifted, -1)
        return ((new_top, total), None)

    upper_start = jnp.full((KEY_VALUE_HEADS, head_groups, token_rows), NEGATIVE_FILL, jnp.float32)
    overall_start = jnp.zeros((KEY_VALUE_HEADS, head_groups, token_rows), jnp.float32)
    (top, total), unused_result = lax.scan(stats, (upper_start, overall_start), block_tiles)
    log_total = top + jnp.log(total)

    def weight_apply(acc, tile):
        masked, allowed = scores(tile)
        probs = jnp.exp(masked - log_total[..., None]).astype(jnp.bfloat16)
        return (
            acc + jnp.einsum("gjqk,kgd->qgjd", probs, tile[1], preferred_element_type=jnp.float32),
            None,
        )

    attention_heads, unused_result = lax.scan(
        weight_apply,
        jnp.zeros((token_rows, KEY_VALUE_HEADS, head_groups, HEAD_SIZE), jnp.float32),
        block_tiles,
    )
    heads_out = attention_heads.reshape(token_rows, QUERY_HEADS * HEAD_SIZE).astype(jnp.bfloat16)
    proj = dot_nt(heads_out, wo_t)
    hidden = inputs + valid_col * proj
    inv_two = lax.rsqrt(jnp.mean(hidden * hidden, -1, keepdims=True) + EPS)
    unit_two = hidden * inv_two
    normed2 = (unit_two * gain_two).astype(jnp.bfloat16)
    normed2_all = gather_tokens(normed2, lanes).reshape(-1, width)
    gate = dot_nn(normed2_all, gate_w)
    up_val = dot_nn(normed2_all, up_w)
    sigma = jax.nn.sigmoid(gate)
    act = (gate * sigma * up_val).astype(jnp.bfloat16)
    d_act = dot_nn(d_down_all, down_w)
    d_gate = (d_act * up_val * sigma * (1.0 + gate * (1.0 - sigma))).astype(jnp.bfloat16)
    d_up = (d_act * gate * sigma).astype(jnp.bfloat16)
    d_n2_parts = dot_nt(d_gate, gate_w) + dot_nt(d_up, up_w)
    d_n2 = scatter_tokens(
        d_n2_parts.astype(jnp.bfloat16).reshape(lanes, token_rows, width), lanes
    )
    down = scatter_tokens(
        dot_nt(act, down_w).astype(jnp.bfloat16).reshape(lanes, token_rows, width), lanes
    )
    mixed = (hidden + valid_col * down).astype(jnp.bfloat16)
    grad_gate = dot_tn(normed2_all, d_gate).astype(jnp.bfloat16)
    grad_up = dot_tn(normed2_all, d_up).astype(jnp.bfloat16)
    grad_down = exchange(
        dot_tn(d_down_all, act).astype(jnp.bfloat16).reshape(lanes, out_part, hidden_part), lanes
    )
    hidden_grads = lax.psum_scatter(
        jnp.concatenate(
            [
                grad_gate.reshape(fsdp_size, rows_each, hidden_part),
                grad_up.reshape(fsdp_size, rows_each, hidden_part),
                grad_down.reshape(fsdp_size, rows_each, hidden_part),
            ],
            1,
        ),
        "fsdp",
        scatter_dimension=0,
        tiled=False,
    ).astype(jnp.float32)
    grad_w_gate = hidden_grads[:rows_each]
    grad_w_up = hidden_grads[rows_each : 2 * rows_each]
    grad_w_down = (
        hidden_grads[2 * rows_each :]
        .reshape(pieces_each, out_part, hidden_part)
        .transpose(0, 2, 1)
        .reshape(-1, out_part)
    )
    scaled_two = d_n2 * gain_two
    dh = grad_out + inv_two * (
        scaled_two - unit_two * jnp.mean(scaled_two * unit_two, -1, keepdims=True)
    )
    grad_gain_two = jnp.sum(d_n2 * unit_two, 0)
    d_proj = (valid_col * dh).astype(jnp.bfloat16)
    out_grad = lax.psum_scatter(
        dot_tn(d_proj, heads_out).astype(jnp.bfloat16).reshape(lanes, out_part, -1),
        "dp",
        scatter_dimension=0,
        tiled=False,
    )
    head_gradient = dot_nn(d_proj, wo_t).astype(jnp.bfloat16)
    head_gradient4 = head_gradient.reshape(token_rows, KEY_VALUE_HEADS, head_groups, HEAD_SIZE)
    delta = jnp.einsum("qgjd,qgjd->gjq", head_gradient4.astype(jnp.float32), attention_heads)

    def attend_reverse(grad_query, tile):
        masked, allowed = scores(tile)
        probs = jnp.exp(masked - log_total[..., None])
        grad_value = jnp.einsum(
            "gjqk,qgjd->kgd",
            probs.astype(jnp.bfloat16),
            head_gradient4,
            preferred_element_type=jnp.float32,
        )
        grad_probs = jnp.einsum(
            "qgjd,kgd->gjqk", head_gradient4, tile[1], preferred_element_type=jnp.float32
        )
        grad_scores = (probs * (grad_probs - delta[..., None])).astype(jnp.bfloat16)
        grad_query = (
            grad_query
            + jnp.einsum("gjqk,kgd->qgjd", grad_scores, tile[0], preferred_element_type=jnp.float32)
            * scale
        )
        grad_key = (
            jnp.einsum(
                "gjqk,qgjd->kgd", grad_scores, query_heads, preferred_element_type=jnp.float32
            )
            * scale
        )
        return (grad_query, (grad_key, grad_value))

    grad_query, (key_gradient, value_gradient) = lax.scan(
        attend_reverse,
        jnp.zeros((token_rows, KEY_VALUE_HEADS, head_groups, HEAD_SIZE), jnp.float32),
        block_tiles,
    )
    own_pair = scatter_rows(
        jnp.concatenate(
            [
                key_gradient.reshape(grouped_rows, KEY_VALUE_HEADS * HEAD_SIZE),
                value_gradient.reshape(grouped_rows, KEY_VALUE_HEADS * HEAD_SIZE),
            ],
            1,
        )
        .astype(jnp.bfloat16)
        .reshape(fsdp_size, token_rows, -1),
        fsdp_size,
    )
    local_keys = own_pair[:, : KEY_VALUE_HEADS * HEAD_SIZE]
    own_values = own_pair[:, KEY_VALUE_HEADS * HEAD_SIZE :]
    d_q_pre = (
        rotary_reverse(grad_query, cosine_table, sine_table)
        .reshape(token_rows, QUERY_HEADS * HEAD_SIZE)
        .astype(jnp.bfloat16)
    )
    d_k_pre = (
        rotary_reverse(
            local_keys.reshape(token_rows, KEY_VALUE_HEADS, HEAD_SIZE), cosine_table, sine_table
        )
        .reshape(token_rows, KEY_VALUE_HEADS * HEAD_SIZE)
        .astype(jnp.bfloat16)
    )
    d_v_pre = own_values.astype(jnp.bfloat16)
    d_joint = jnp.concatenate([d_q_pre, d_k_pre, d_v_pre], 1)
    d_n1 = dot_nn(d_joint, joint_t)
    scaled_one = d_n1 * gain_one
    d_tokens = (
        dh + inv_one * (scaled_one - unit_one * jnp.mean(scaled_one * unit_one, -1, keepdims=True))
    ).astype(jnp.bfloat16)
    grad_gain_one = jnp.sum(d_n1 * unit_one, 0)
    local_vectors = (
        grad_gain_one,
        jnp.sum(d_q_pre.astype(jnp.float32), 0),
        jnp.sum(d_v_pre.astype(jnp.float32), 0),
        grad_gain_two,
    )
    vector_rows = jnp.concatenate([v.reshape(lanes, -1) for v in local_vectors], 1)
    vector_rows = jnp.pad(vector_rows, ((0, 0), (0, width - vector_count)))
    vector_rows = jnp.pad(vector_rows[:, None].astype(jnp.bfloat16), ((0, 0), (0, 15), (0, 0)))
    joint_grads = dot_tn(d_joint, normed).astype(jnp.bfloat16)
    joint_sum = lax.psum_scatter(
        jnp.concatenate(
            [
                joint_grads[:query_width].reshape(lanes, query_part, width),
                joint_grads[query_width : query_width + key_width].reshape(lanes, key_part, width),
                joint_grads[query_width + key_width :].reshape(lanes, key_part, width),
                vector_rows,
            ],
            1,
        ),
        "dp",
        scatter_dimension=0,
        tiled=False,
    )
    qkv_rows = query_part + 2 * key_part
    row_sums = scatter_rows(
        jnp.concatenate([joint_sum[:qkv_rows], out_grad])
        .T.reshape(fsdp_size, rows_each, joint_rows),
        fsdp_size,
    )
    grad_w_query, grad_w_key, grad_w_value, out_grad = [
        row_sums[:, edges[i] : edges[i + 1]] for i in range(4)
    ]
    own_vectors = joint_sum[qkv_rows, :vector_count].astype(jnp.float32)
    vector_sum = own_vectors
    for k in range(1, fsdp_size):
        vector_sum = vector_sum + lax.ppermute(
            own_vectors, "fsdp", [(i, (i + k) % fsdp_size) for i in range(fsdp_size)]
        )
    vector_pieces = [vector_sum[marks[i] : marks[i + 1]] for i in range(4)]
    return (
        mixed[None],
        d_tokens[None],
        vector_pieces[0],
        grad_w_query,
        vector_pieces[1],
        grad_w_key,
        grad_w_value,
        vector_pieces[2],
        out_grad,
        vector_pieces[3],
        grad_w_gate,
        grad_w_up,
        grad_w_down,
    )


def solution(mesh):
    placed = (
        P("dp", "fsdp", None),
        P("dp", "fsdp", None),
        P("dp", None),
        P("dp", None),
        P("dp"),
        P("fsdp", "dp"),
        P("dp"),
        P("fsdp", "dp"),
        P("fsdp", "dp"),
        P("dp"),
        P("fsdp", "dp"),
        P("dp"),
        P("fsdp", "dp"),
        P("fsdp", "dp"),
        P("fsdp", "dp"),
    )
    return jax.shard_map(
        body,
        mesh=mesh,
        in_specs=placed,
        out_specs=(
            P("dp", "fsdp", None),
            P("dp", "fsdp", None),
            P("dp"),
            P("fsdp", "dp"),
            P("dp"),
            P("fsdp", "dp"),
            P("fsdp", "dp"),
            P("dp"),
            P("fsdp", "dp"),
            P("dp"),
            P("fsdp", "dp"),
            P("fsdp", "dp"),
            P("fsdp", "dp"),
        ),
        check_vma=False,
    )
```

```python
import jax
import jax.numpy as jnp
from jax import lax
from jax.experimental import pallas as pl
from jax.experimental.pallas import tpu as pltpu
from jax.sharding import PartitionSpec as P

QUERY_HEADS = 14
KEY_VALUE_HEADS = 2
HEAD_SIZE = 64
KERNEL_BYTES = 48 * 2**20


EPS = 1e-06
THETA = 1000000.0
NEGATIVE_FILL = -1e30


def own_slots(count_row, length_row, place, slots):
    before = jnp.cumsum(count_row) - count_row
    inner = jnp.arange(slots, dtype=jnp.int32)
    valid = inner < count_row[place]
    index = before[place] + inner
    ends = jnp.cumsum(length_row)
    numbers = jnp.sum((index[:, None] >= ends[None, :]).astype(jnp.int32), 1)
    starts = ends - length_row
    owners = jnp.arange(length_row.shape[0], dtype=jnp.int32)
    start_of = jnp.sum(
        (numbers[:, None] == owners[None, :]).astype(jnp.int32) * starts[None, :], 1
    )
    position = jnp.where(valid, index - start_of, 0)
    opened = jnp.max(jnp.where(index[:, None] >= ends[None, :], ends[None, :], 0), 1)
    low = jnp.where(valid, opened, 0)
    high = jnp.where(valid, index, 0)
    return valid, position, low, high, jnp.stack([count_row, before])


def rope_tables(position, half):
    steps = jnp.arange(half, dtype=jnp.float32) * (1.0 / half)
    freq = THETA ** (-steps)
    angle = freq[:, None] * position[None, :]
    return jnp.cos(angle), jnp.sin(angle)


def rotary_apply(rows, cosine, sine):
    cube = rows.reshape(-1, 2, HEAD_SIZE // 2, rows.shape[1])
    first, second = cube[:, 0], cube[:, 1]
    turned = [first * cosine - second * sine, second * cosine + first * sine]
    return jnp.stack(turned, 1).reshape(rows.shape)


def rotary_reverse(rows, cosine, sine):
    return rotary_apply(rows, cosine, -sine)


def flip(array, mask, size):
    return lax.ppermute(array, "dp", [(i, i ^ mask) for i in range(size)])


def gather_tokens(rows, size):
    if size != 8:
        return lax.all_gather(rows, "dp", axis=0)
    half = rows.shape[0] // 2
    by_x, by_y, by_core = flip(rows, 2, 8), flip(rows, 4, 8), flip(rows, 1, 8)
    far_a, far_b = flip(by_x[:half], 4, 8), flip(by_y[half:], 2, 8)
    core_x, core_y = flip(by_x, 1, 8), flip(by_y, 1, 8)
    core_a, core_b = flip(far_a, 1, 8), flip(far_b, 1, 8)
    return jnp.stack(
        [
            rows,
            by_core,
            by_x,
            core_x,
            by_y,
            core_y,
            jnp.concatenate([far_a, far_b]),
            jnp.concatenate([core_a, core_b]),
        ]
    )


def ordered_blocks(blocks, size):
    if size != 8:
        return blocks
    place = lax.axis_index("dp")
    result = blocks
    for k in range(8):
        result = lax.dynamic_update_slice_in_dim(result, blocks[k : k + 1], place ^ k, 0)
    return result


def scatter_tokens(parts, size, ordered=False):
    if size != 8:
        return lax.psum_scatter(
            parts.astype(jnp.bfloat16), "dp", scatter_dimension=0, tiled=False
        ).astype(jnp.float32)
    if ordered:
        place = lax.axis_index("dp")
        parts = [lax.dynamic_index_in_dim(parts, place ^ k, 0, False) for k in range(8)]
    sent = [part.astype(jnp.bfloat16) for part in parts]
    half = parts[0].shape[0] // 2
    wide = jnp.float32
    seven, five, three, one = [flip(sent[k], 1, 8) for k in (7, 5, 3, 1)]
    far = (parts[6].astype(wide) + seven.astype(wide)).astype(jnp.bfloat16)
    far_x, far_y = flip(far[:half], 2, 8), flip(far[half:], 4, 8)
    on_y = parts[4].astype(wide) + five.astype(wide)
    on_x = parts[2].astype(wide) + three.astype(wide)
    on_y = jnp.concatenate([on_y[:half] + far_x.astype(wide), on_y[half:]]).astype(jnp.bfloat16)
    on_x = jnp.concatenate([on_x[:half], on_x[half:] + far_y.astype(wide)]).astype(jnp.bfloat16)
    got_x, got_y = flip(on_x, 2, 8), flip(on_y, 4, 8)
    own = parts[0].astype(wide) + one.astype(wide)
    return own + got_x.astype(wide) + got_y.astype(wide)


def exchange(parts, size):
    if size != 8:
        return lax.all_to_all(parts, "dp", 0, 0, tiled=True)
    place = lax.axis_index("dp")
    block = parts.reshape((2, 2, 2) + parts.shape[1:])
    for axis, mask in ((2, 1), (1, 2), (0, 4)):
        mine = (place // mask) % 2
        kept = lax.dynamic_index_in_dim(block, mine, axis, True)
        got = flip(lax.dynamic_index_in_dim(block, 1 - mine, axis, True), mask, 8)
        both = jnp.concatenate([kept, got], axis)
        swapped = jnp.concatenate([got, kept], axis)
        block = jnp.where(mine == 0, both, swapped)
    return block.reshape(parts.shape)


def gather_rows(rows, size):
    place = lax.axis_index("fsdp")
    result = jnp.zeros((size,) + rows.shape, rows.dtype)
    result = lax.dynamic_update_slice_in_dim(result, rows[None], place, 0)
    for k in range(1, size):
        piece = lax.ppermute(rows, "fsdp", [(i, (i + k) % size) for i in range(size)])
        result = lax.dynamic_update_slice_in_dim(result, piece[None], (place + size - k) % size, 0)
    return result


def scatter_rows(parts, size):
    place = lax.axis_index("fsdp")
    sent = parts.astype(jnp.bfloat16)
    total = lax.dynamic_index_in_dim(parts, place, 0, False).astype(jnp.float32)
    for k in range(1, size):
        piece = lax.dynamic_index_in_dim(sent, (place + k) % size, 0, False)
        total = total + lax.ppermute(
            piece, "fsdp", [(i, (i + k) % size) for i in range(size)]
        ).astype(jnp.float32)
    return total


def dot_tn(left, right):
    return lax.dot_general(
        left, right, (((0,), (0,)), ((), ())), preferred_element_type=jnp.float32
    )


def dot_nt(left, right):
    return lax.dot_general(
        left, right, (((1,), (1,)), ((), ())), preferred_element_type=jnp.float32
    )


def dot_nn(left, right):
    return jnp.dot(left, right, preferred_element_type=jnp.float32)


def pick_rows(meta_ref, e, slots, kept):
    slot = lax.broadcasted_iota(jnp.int32, (slots, kept), 0)
    index = lax.broadcasted_iota(jnp.int32, (slots, kept), 1)
    chosen = (slot + meta_ref[1, e] == index) & (slot < meta_ref[0, e])
    return jnp.where(chosen, 1.0, 0.0).astype(jnp.bfloat16)


def range_bias(low_ref, high_ref, kept, rows):
    index = lax.broadcasted_iota(jnp.int32, (kept, rows), 0)
    inside = (index >= low_ref[...]) & (index <= high_ref[...])
    return jnp.where(inside, 0.0, NEGATIVE_FILL)


def attend_kernel(
    meta_ref, low_ref, high_ref, q_ref, kv_ref, o_ref, attn_ref, lse_ref, kvc_ref, bias_ref, k_ref
):
    shards, both, slots = kv_ref.shape
    kept, rows = bias_ref.shape
    head_groups = QUERY_HEADS // KEY_VALUE_HEADS
    key_width = both // 2
    packed = jnp.zeros((both, kept), jnp.float32)
    for e in range(shards):
        packed = packed + jnp.dot(
            kv_ref[e], pick_rows(meta_ref, e, slots, kept), preferred_element_type=jnp.float32
        )
    kvc_ref[...] = packed.astype(jnp.bfloat16)
    for g in range(KEY_VALUE_HEADS):
        k_ref[g] = packed[g * HEAD_SIZE : (g + 1) * HEAD_SIZE].T.astype(jnp.bfloat16)
    bias_ref[...] = range_bias(low_ref, high_ref, kept, rows)

    def pair(c, carry):
        found = []
        for j in range(2):
            h = 2 * c + j
            g = h // head_groups
            at = pl.multiple_of(h * HEAD_SIZE, HEAD_SIZE)
            s = jnp.dot(
                k_ref[g], q_ref[pl.ds(at, HEAD_SIZE), :], preferred_element_type=jnp.float32
            )
            s = s + bias_ref[...]
            top = jnp.max(s, 0, keepdims=True)
            p = jnp.exp(s - top)
            total = jnp.sum(p, 0, keepdims=True)
            v_at = pl.multiple_of(key_width + g * HEAD_SIZE, HEAD_SIZE)
            out = jnp.dot(
                kvc_ref[pl.ds(v_at, HEAD_SIZE), :],
                p.astype(jnp.bfloat16),
                preferred_element_type=jnp.float32,
            )
            out = out / total
            attn_ref[pl.ds(at, HEAD_SIZE), :] = out
            lse_ref[h] = top + jnp.log(total)
            found.append(out)
        block = jnp.concatenate(found, 0).T
        o_ref[:, pl.ds(pl.multiple_of(c * 2 * HEAD_SIZE, 2 * HEAD_SIZE), 2 * HEAD_SIZE)] = (
            block.astype(jnp.bfloat16)
        )
        return carry

    lax.fori_loop(0, QUERY_HEADS // 2, pair, 0)


def attend(meta, low, high, q, kv):
    shards, both, slots = kv.shape
    kept = shards * slots * 3 // 4
    width, rows = q.shape
    whole = pl.BlockSpec(memory_space=pltpu.VMEM)
    return pl.pallas_call(
        attend_kernel,
        out_shape=(
            jax.ShapeDtypeStruct((rows, width), jnp.bfloat16),
            jax.ShapeDtypeStruct((width, rows), jnp.float32),
            jax.ShapeDtypeStruct((QUERY_HEADS, 1, rows), jnp.float32),
            jax.ShapeDtypeStruct((both, kept), jnp.bfloat16),
        ),
        in_specs=[pl.BlockSpec(memory_space=pltpu.SMEM)] + [whole] * 4,
        out_specs=(whole,) * 4,
        scratch_shapes=[
            pltpu.VMEM((kept, rows), jnp.float32),
            pltpu.VMEM((KEY_VALUE_HEADS, kept, HEAD_SIZE), jnp.bfloat16),
        ],
        compiler_params=pltpu.CompilerParams(vmem_limit_bytes=KERNEL_BYTES),
        cost_estimate=pl.CostEstimate(
            flops=4 * width * rows * kept * 4,
            bytes_accessed=width * rows * 8,
            transcendentals=QUERY_HEADS * rows * kept,
        ),
        name="attend",
    )(meta, low, high, q, kv)


def attend_back_kernel(
    meta_ref,
    low_ref,
    high_ref,
    q_ref,
    kvc_ref,
    d_o_ref,
    attn_ref,
    lse_ref,
    d_q_ref,
    d_kv_ref,
    bias_ref,
    k_ref,
    v_ref,
    d_k_ref,
    d_v_ref,
):
    shards, both, slots = d_kv_ref.shape
    kept, rows = bias_ref.shape
    head_groups = QUERY_HEADS // KEY_VALUE_HEADS
    key_width = both // 2
    for g in range(KEY_VALUE_HEADS):
        k_ref[g] = kvc_ref[g * HEAD_SIZE : (g + 1) * HEAD_SIZE, :].astype(jnp.float32).T.astype(jnp.bfloat16)
        v_ref[g] = (
            kvc_ref[key_width + g * HEAD_SIZE : key_width + (g + 1) * HEAD_SIZE, :]
            .astype(jnp.float32)
            .T.astype(jnp.bfloat16)
        )
    bias_ref[...] = range_bias(low_ref, high_ref, kept, rows)
    d_k_ref[...] = jnp.zeros_like(d_k_ref)
    d_v_ref[...] = jnp.zeros_like(d_v_ref)

    def pair(c, carry):
        d_o_pair = d_o_ref[:, pl.ds(pl.multiple_of(c * 2 * HEAD_SIZE, 2 * HEAD_SIZE), 2 * HEAD_SIZE)]
        d_o_wide = d_o_pair.astype(jnp.float32).T
        pair_at = pl.multiple_of(c * 2 * HEAD_SIZE, 2 * HEAD_SIZE)
        q_rows = q_ref[pl.ds(pair_at, 2 * HEAD_SIZE), :].astype(jnp.float32).T.astype(jnp.bfloat16)
        for j in range(2):
            h = 2 * c + j
            g = h // head_groups
            at = pl.multiple_of(h * HEAD_SIZE, HEAD_SIZE)
            part = slice(j * HEAD_SIZE, (j + 1) * HEAD_SIZE)
            d_o_t = d_o_wide[part]
            delta = jnp.sum(d_o_t * attn_ref[pl.ds(at, HEAD_SIZE), :], 0, keepdims=True)
            s = jnp.dot(
                k_ref[g], q_ref[pl.ds(at, HEAD_SIZE), :], preferred_element_type=jnp.float32
            )
            p = jnp.exp(s + bias_ref[...] - lse_ref[h])
            d_p = jnp.dot(
                v_ref[g], d_o_t.astype(jnp.bfloat16), preferred_element_type=jnp.float32
            )
            d_s = (p * (d_p - delta)).astype(jnp.bfloat16)
            d_v_ref[g] += jnp.dot(
                p.astype(jnp.bfloat16), d_o_pair[:, part], preferred_element_type=jnp.float32
            )
            d_k_ref[g] += jnp.dot(d_s, q_rows[:, part], preferred_element_type=jnp.float32)
            k_at = pl.multiple_of(g * HEAD_SIZE, HEAD_SIZE)
            d_q_ref[pl.ds(at, HEAD_SIZE), :] = (
                jnp.dot(
                    kvc_ref[pl.ds(k_at, HEAD_SIZE), :], d_s, preferred_element_type=jnp.float32
                )
                * HEAD_SIZE**-0.5
            )
        return carry

    lax.fori_loop(0, QUERY_HEADS // 2, pair, 0)
    halves = [d_k_ref[g].T for g in range(KEY_VALUE_HEADS)]
    halves = halves + [d_v_ref[g].T for g in range(KEY_VALUE_HEADS)]
    packed = jnp.concatenate(halves, 0).astype(jnp.bfloat16)
    for e in range(shards):
        d_kv_ref[e] = lax.dot_general(
            packed,
            pick_rows(meta_ref, e, slots, kept),
            (((1,), (1,)), ((), ())),
            preferred_element_type=jnp.float32,
        ).astype(jnp.bfloat16)


def attend_back(meta, low, high, q, kvc, d_o, attn, lse):
    both, kept = kvc.shape
    width, rows = q.shape
    shards = meta.shape[1]
    whole = pl.BlockSpec(memory_space=pltpu.VMEM)
    per_head = (KEY_VALUE_HEADS, kept, HEAD_SIZE)
    return pl.pallas_call(
        attend_back_kernel,
        out_shape=(
            jax.ShapeDtypeStruct((width, rows), jnp.float32),
            jax.ShapeDtypeStruct((shards, both, rows), jnp.bfloat16),
        ),
        in_specs=[pl.BlockSpec(memory_space=pltpu.SMEM)] + [whole] * 7,
        out_specs=(whole,) * 2,
        scratch_shapes=[
            pltpu.VMEM((kept, rows), jnp.float32),
            pltpu.VMEM(per_head, jnp.bfloat16),
            pltpu.VMEM(per_head, jnp.bfloat16),
            pltpu.VMEM(per_head, jnp.float32),
            pltpu.VMEM(per_head, jnp.float32),
        ],
        compiler_params=pltpu.CompilerParams(vmem_limit_bytes=KERNEL_BYTES),
        cost_estimate=pl.CostEstimate(
            flops=10 * width * rows * kept * 4,
            bytes_accessed=width * rows * 12,
            transcendentals=QUERY_HEADS * rows * kept,
        ),
        name="attend_back",
    )(meta, low, high, q, kvc, d_o, attn, lse)


def body(
    tokens,
    cotangent,
    counts,
    lengths,
    attn_gain,
    w_query,
    b_query,
    w_key,
    w_value,
    b_value,
    w_out,
    mlp_gain,
    w_gate,
    w_up,
    w_down,
):
    lanes = lax.axis_size("dp")
    fsdp_size = lax.axis_size("fsdp")
    token_rows, width = tokens.shape[1:]
    inputs = tokens[0].astype(jnp.float32)
    valid, position, low, high, meta = own_slots(
        counts[0], lengths[0], lax.axis_index("fsdp"), token_rows
    )
    valid_col = valid.astype(jnp.float32)[:, None]
    query_part, key_part, out_part = w_query.shape[1], w_key.shape[1], w_out.shape[1]
    hidden_part = w_gate.shape[1]
    pieces_each = lanes // fsdp_size
    query_width, key_width = QUERY_HEADS * HEAD_SIZE, KEY_VALUE_HEADS * HEAD_SIZE
    rows_each = w_gate.shape[0]

    projections = (
        gather_rows(jnp.concatenate([w_query, w_key, w_value, w_out], 1), fsdp_size)
        .reshape(width, -1)
        .T
    )
    joint_rows = projections.shape[0]
    vector_row = jnp.concatenate([attn_gain, b_query, b_value, mlp_gain])
    vector_count = vector_row.shape[0]
    vector_block = jnp.zeros((16, width), jnp.bfloat16).at[0, :vector_count].set(vector_row)
    spread = ordered_blocks(
        gather_tokens(jnp.concatenate([projections, vector_block]), lanes), lanes
    )
    edges = (0, query_part, query_part + key_part, query_part + 2 * key_part, joint_rows)
    wq_t, wk_t, wv_t, wo_t = [
        spread[:, edges[i] : edges[i + 1]].reshape(-1, width) for i in range(4)
    ]
    joint_t = jnp.concatenate([wq_t, wk_t, wv_t])
    vector_table = spread[:, joint_rows, :vector_count].astype(jnp.float32)
    marks = [0]
    for size in (query_part, query_part, key_part, query_part):
        marks.append(marks[-1] + size)
    gain_one, query_bias, value_bias, gain_two = [
        vector_table[:, marks[i] : marks[i + 1]].reshape(-1) for i in range(4)
    ]

    down_t = w_down.T.reshape(out_part, pieces_each, hidden_part).transpose(1, 0, 2)
    hidden_own = jnp.concatenate([w_gate, w_up, down_t.reshape(-1, hidden_part)])
    hidden_own, projections = lax.optimization_barrier((hidden_own, projections))
    hidden_slabs = lax.all_gather(hidden_own, "fsdp", axis=0)
    gate_w = hidden_slabs[:, :rows_each].reshape(width, hidden_part)
    up_w = hidden_slabs[:, rows_each : 2 * rows_each].reshape(width, hidden_part)
    down_w = exchange(
        hidden_slabs[:, 2 * rows_each :].reshape(lanes, out_part, hidden_part), lanes
    ).reshape(width, hidden_part)
    grad_out = cotangent[0].astype(jnp.float32)
    d_down, joint_t = lax.optimization_barrier(
        ((valid_col * grad_out).astype(jnp.bfloat16), joint_t)
    )
    d_down_all = gather_tokens(d_down, lanes).reshape(-1, width)

    inv_one = lax.rsqrt(jnp.mean(inputs * inputs, -1, keepdims=True) + EPS)
    unit_one = inputs * inv_one
    normed = (unit_one * gain_one).astype(jnp.bfloat16)
    joint = dot_nt(joint_t, normed)
    cosine, sine = rope_tables(position.astype(jnp.float32), HEAD_SIZE // 2)
    query_rows = rotary_apply(joint[:query_width] + query_bias[:, None], cosine, sine)
    query_rows = query_rows.astype(jnp.bfloat16) * jnp.bfloat16(HEAD_SIZE**-0.5)
    key_rows = rotary_apply(joint[query_width : query_width + key_width], cosine, sine)
    value_rows = joint[query_width + key_width :] + value_bias[:, None]
    gathered = gather_rows(
        jnp.concatenate([key_rows, value_rows]).astype(jnp.bfloat16), fsdp_size
    )
    heads_out, attention, log_total, packed_kv = attend(
        meta, low[None], high[None], query_rows, gathered
    )
    proj = dot_nt(heads_out, wo_t)
    hidden = inputs + valid_col * proj
    inv_two = lax.rsqrt(jnp.mean(hidden * hidden, -1, keepdims=True) + EPS)
    unit_two = hidden * inv_two
    normed2 = (unit_two * gain_two).astype(jnp.bfloat16)

    normed2_all = gather_tokens(normed2, lanes).reshape(-1, width)
    gate = dot_nn(normed2_all, gate_w)
    up_val = dot_nn(normed2_all, up_w)
    sigma = jax.nn.sigmoid(gate)
    act = (gate * sigma * up_val).astype(jnp.bfloat16)
    d_act = dot_nn(d_down_all, down_w)
    d_gate = (d_act * up_val * sigma * (1.0 + gate * (1.0 - sigma))).astype(jnp.bfloat16)
    d_up = (d_act * gate * sigma).astype(jnp.bfloat16)
    d_n2_parts = dot_nt(d_gate, gate_w) + dot_nt(d_up, up_w)
    d_n2 = scatter_tokens(
        d_n2_parts.astype(jnp.bfloat16).reshape(lanes, token_rows, width), lanes
    )
    down = scatter_tokens(
        dot_nt(act, down_w).astype(jnp.bfloat16).reshape(lanes, token_rows, width), lanes
    )
    mixed = (hidden + valid_col * down).astype(jnp.bfloat16)
    grad_gate = dot_tn(normed2_all, d_gate).astype(jnp.bfloat16)
    grad_up = dot_tn(normed2_all, d_up).astype(jnp.bfloat16)
    grad_down = dot_tn(d_down_all, act).astype(jnp.bfloat16)
    pair_grads = jnp.concatenate(
        [
            grad_gate.reshape(fsdp_size, rows_each, hidden_part),
            grad_up.reshape(fsdp_size, rows_each, hidden_part),
        ],
        1,
    )

    scaled_two = d_n2 * gain_two
    dh = grad_out + inv_two * (
        scaled_two - unit_two * jnp.mean(scaled_two * unit_two, -1, keepdims=True)
    )
    grad_gain_two = jnp.sum(d_n2 * unit_two, 0)
    d_proj = (valid_col * dh).astype(jnp.bfloat16)
    d_proj, pair_grads, grad_down = lax.optimization_barrier((d_proj, pair_grads, grad_down))
    pair_sums = lax.psum_scatter(
        pair_grads, "fsdp", scatter_dimension=0, tiled=False
    ).astype(jnp.float32)
    grad_w_gate = pair_sums[:rows_each]
    grad_w_up = pair_sums[rows_each:]
    grad_down = exchange(grad_down.reshape(lanes, out_part, hidden_part), lanes)
    grad_w_down = (
        lax.psum_scatter(
            grad_down.reshape(fsdp_size, rows_each, hidden_part),
            "fsdp",
            scatter_dimension=0,
            tiled=False,
        )
        .astype(jnp.float32)
        .reshape(pieces_each, out_part, hidden_part)
        .transpose(0, 2, 1)
        .reshape(-1, out_part)
    )
    out_grad = lax.psum_scatter(
        dot_tn(d_proj, heads_out).astype(jnp.bfloat16).reshape(lanes, out_part, -1),
        "dp",
        scatter_dimension=0,
        tiled=False,
    )
    head_gradient = dot_nn(d_proj, wo_t).astype(jnp.bfloat16)
    d_query, d_kv = attend_back(
        meta, low[None], high[None], query_rows, packed_kv, head_gradient, attention, log_total
    )
    own_kv = scatter_rows(d_kv, fsdp_size)
    d_q_pre = rotary_reverse(d_query, cosine, sine).astype(jnp.bfloat16)
    d_k_pre = rotary_reverse(own_kv[:key_width], cosine, sine).astype(jnp.bfloat16)
    d_v_pre = own_kv[key_width:].astype(jnp.bfloat16)
    d_joint = jnp.concatenate([d_q_pre, d_k_pre, d_v_pre])
    d_n1 = dot_tn(d_joint, joint_t)
    scaled_one = d_n1 * gain_one
    d_tokens = (
        dh + inv_one * (scaled_one - unit_one * jnp.mean(scaled_one * unit_one, -1, keepdims=True))
    ).astype(jnp.bfloat16)
    local_vectors = (
        jnp.sum(d_n1 * unit_one, 0),
        jnp.sum(d_q_pre.astype(jnp.float32), 1),
        jnp.sum(d_v_pre.astype(jnp.float32), 1),
        grad_gain_two,
    )
    vector_rows = jnp.concatenate([v.reshape(lanes, -1) for v in local_vectors], 1)
    vector_rows = jnp.pad(vector_rows, ((0, 0), (0, width - vector_count)))
    vector_rows = jnp.pad(vector_rows[:, None].astype(jnp.bfloat16), ((0, 0), (0, 15), (0, 0)))
    joint_grads = dot_nn(d_joint, normed).astype(jnp.bfloat16)
    joint_sum = scatter_tokens(
        jnp.concatenate(
            [
                joint_grads[:query_width].reshape(lanes, query_part, width),
                joint_grads[query_width : query_width + key_width].reshape(lanes, key_part, width),
                joint_grads[query_width + key_width :].reshape(lanes, key_part, width),
                vector_rows,
            ],
            1,
        ),
        lanes,
        ordered=True,
    )
    qkv_rows = query_part + 2 * key_part
    row_sums = scatter_rows(
        jnp.concatenate([joint_sum[:qkv_rows].astype(jnp.bfloat16), out_grad])
        .T.reshape(fsdp_size, rows_each, joint_rows),
        fsdp_size,
    )
    grad_w_query, grad_w_key, grad_w_value, out_grad = [
        row_sums[:, edges[i] : edges[i + 1]] for i in range(4)
    ]
    own_vectors = joint_sum[qkv_rows, :vector_count]
    vector_sum = own_vectors
    for k in range(1, fsdp_size):
        vector_sum = vector_sum + lax.ppermute(
            own_vectors, "fsdp", [(i, (i + k) % fsdp_size) for i in range(fsdp_size)]
        )
    vector_pieces = [vector_sum[marks[i] : marks[i + 1]] for i in range(4)]
    return (
        mixed[None],
        d_tokens[None],
        vector_pieces[0],
        grad_w_query,
        vector_pieces[1],
        grad_w_key,
        grad_w_value,
        vector_pieces[2],
        out_grad,
        vector_pieces[3],
        grad_w_gate,
        grad_w_up,
        grad_w_down,
    )


def solution(mesh):
    placed = (
        P("dp", "fsdp", None),
        P("dp", "fsdp", None),
        P("dp", None),
        P("dp", None),
        P("dp"),
        P("fsdp", "dp"),
        P("dp"),
        P("fsdp", "dp"),
        P("fsdp", "dp"),
        P("dp"),
        P("fsdp", "dp"),
        P("dp"),
        P("fsdp", "dp"),
        P("fsdp", "dp"),
        P("fsdp", "dp"),
    )
    return jax.shard_map(
        body,
        mesh=mesh,
        in_specs=placed,
        out_specs=(
            P("dp", "fsdp", None),
            P("dp", "fsdp", None),
            P("dp"),
            P("fsdp", "dp"),
            P("dp"),
            P("fsdp", "dp"),
            P("fsdp", "dp"),
            P("dp"),
            P("fsdp", "dp"),
            P("dp"),
            P("fsdp", "dp"),
            P("fsdp", "dp"),
            P("fsdp", "dp"),
        ),
        check_vma=False,
    )
```

```python
import functools

import jax
import jax.numpy as jnp
from jax import lax
from jax.experimental import pallas as pl
from jax.experimental.pallas import tpu as pltpu
from jax.sharding import PartitionSpec as P

QUERY_HEADS = 14
KEY_VALUE_HEADS = 2
HEAD_SIZE = 64
KERNEL_BYTES = 24 * 2**20
ATTEND_BYTES = 32 * 2**20


EPS = 1e-06
THETA = 1000000.0
NEGATIVE_FILL = -1e30


def own_slots(count_row, length_row, place, slots):
    before = jnp.cumsum(count_row) - count_row
    inner = jnp.arange(slots, dtype=jnp.int32)
    valid = inner < count_row[place]
    index = before[place] + inner
    ends = jnp.cumsum(length_row)
    numbers = jnp.sum((index[:, None] >= ends[None, :]).astype(jnp.int32), 1)
    starts = ends - length_row
    owners = jnp.arange(length_row.shape[0], dtype=jnp.int32)
    start_of = jnp.sum(
        (numbers[:, None] == owners[None, :]).astype(jnp.int32) * starts[None, :], 1
    )
    position = jnp.where(valid, index - start_of, 0)
    opened = jnp.max(jnp.where(index[:, None] >= ends[None, :], ends[None, :], 0), 1)
    low = jnp.where(valid, opened, 0)
    high = jnp.where(valid, index, 0)
    return valid, position, low, high, jnp.stack([count_row, before])


def rope_tables(position, half):
    steps = jnp.arange(half, dtype=jnp.float32) * (1.0 / half)
    freq = THETA ** (-steps)
    angle = freq[:, None] * position[None, :]
    return jnp.cos(angle), jnp.sin(angle)


def rotary_apply(rows, cosine, sine):
    cube = rows.reshape(-1, 2, HEAD_SIZE // 2, rows.shape[1])
    first, second = cube[:, 0], cube[:, 1]
    turned = [first * cosine - second * sine, second * cosine + first * sine]
    return jnp.stack(turned, 1).reshape(rows.shape)


def rotary_reverse(rows, cosine, sine):
    return rotary_apply(rows, cosine, -sine)


def flip(array, mask, size):
    return lax.ppermute(array, "dp", [(i, i ^ mask) for i in range(size)])


def tie(first, second):
    return lax.optimization_barrier((first, second))


def finish(steps, pending):
    try:
        steps.send(pending)
    except StopIteration as end:
        return end.value


def run(steps):
    try:
        pending = next(steps)
        while True:
            pending = steps.send(pending[0])
    except StopIteration as end:
        return end.value


def gather_steps(rows, size):
    if size != 8:
        whole = lax.all_gather(rows, "dp", axis=0)
        pieces = [whole[k] for k in range(size)]
        yield (), pieces[:2]
        yield (), pieces[2 : size - 2]
        return pieces
    half = rows.shape[0] // 2
    by_x, by_y, by_core = flip(rows, 2, 8), flip(rows, 4, 8), flip(rows, 1, 8)
    by_x, by_y = yield (by_x, by_y), [rows, by_core]
    far_a, far_b = flip(by_x[:half], 4, 8), flip(by_y[half:], 2, 8)
    core_x, core_y = flip(by_x, 1, 8), flip(by_y, 1, 8)
    far_a, far_b = yield (far_a, far_b), [by_x, core_x, by_y, core_y]
    far = jnp.concatenate([far_a, far_b])
    return [rows, by_core, by_x, core_x, by_y, core_y, far, flip(far, 1, 8)]


def scatter_steps(parts, size, ordered=False):
    if size != 8:
        total = lax.psum_scatter(jnp.stack(parts), "dp", scatter_dimension=0, tiled=False)
        yield (), None
        yield (), None
        return total.astype(jnp.float32)
    if ordered:
        place = lax.axis_index("dp")
        parts = jnp.stack(parts)
        parts = [lax.dynamic_index_in_dim(parts, place ^ k, 0, False) for k in range(8)]
    half = parts[0].shape[0] // 2
    wide = jnp.float32
    seven, five, three, one = [flip(parts[k], 1, 8) for k in (7, 5, 3, 1)]
    far = (parts[6].astype(wide) + seven.astype(wide)).astype(jnp.bfloat16)
    far_x, far_y = yield (flip(far[:half], 2, 8), flip(far[half:], 4, 8)), None
    on_y = parts[4].astype(wide) + five.astype(wide)
    on_x = parts[2].astype(wide) + three.astype(wide)
    on_y = jnp.concatenate([on_y[:half] + far_x.astype(wide), on_y[half:]]).astype(jnp.bfloat16)
    on_x = jnp.concatenate([on_x[:half], on_x[half:] + far_y.astype(wide)]).astype(jnp.bfloat16)
    got_x, got_y = yield (flip(on_x, 2, 8), flip(on_y, 4, 8)), None
    own = parts[0].astype(wide) + one.astype(wide)
    return own + got_x.astype(wide) + got_y.astype(wide)


def exchange_steps(parts, size):
    if size != 8:
        result = lax.all_to_all(parts, "dp", 0, 0, tiled=True)
        yield (), None
        yield (), None
        return result
    place = lax.axis_index("dp")
    block = parts.reshape((2, 2, 2) + parts.shape[1:])
    for axis, mask in ((2, 1), (1, 2), (0, 4)):
        mine = (place // mask) % 2
        kept = lax.dynamic_index_in_dim(block, mine, axis, True)
        got = flip(lax.dynamic_index_in_dim(block, 1 - mine, axis, True), mask, 8)
        if mask > 1:
            got = yield got, None
        both = jnp.concatenate([kept, got], axis)
        swapped = jnp.concatenate([got, kept], axis)
        block = jnp.where(mine == 0, both, swapped)
    return block.reshape(parts.shape)


def gather_rows(rows, size):
    place = lax.axis_index("fsdp")
    result = jnp.zeros((size,) + rows.shape, rows.dtype)
    result = lax.dynamic_update_slice_in_dim(result, rows[None], place, 0)
    for k in range(1, size):
        piece = lax.ppermute(rows, "fsdp", [(i, (i + k) % size) for i in range(size)])
        result = lax.dynamic_update_slice_in_dim(result, piece[None], (place + size - k) % size, 0)
    return result


def scatter_rows(parts, size):
    place = lax.axis_index("fsdp")
    sent = parts.astype(jnp.bfloat16)
    total = lax.dynamic_index_in_dim(parts, place, 0, False).astype(jnp.float32)
    for k in range(1, size):
        piece = lax.dynamic_index_in_dim(sent, (place + k) % size, 0, False)
        total = total + lax.ppermute(
            piece, "fsdp", [(i, (i + k) % size) for i in range(size)]
        ).astype(jnp.float32)
    return total


def dot_tn(left, right):
    return lax.dot_general(
        left, right, (((0,), (0,)), ((), ())), preferred_element_type=jnp.float32
    )


def dot_nt(left, right):
    return lax.dot_general(
        left, right, (((1,), (1,)), ((), ())), preferred_element_type=jnp.float32
    )


def dot_nn(left, right):
    return jnp.dot(left, right, preferred_element_type=jnp.float32)


def assemble_kernel(place_ref, *refs):
    pieces, (joint_ref, out_ref, vector_ref) = refs[:8], refs[8:]
    width = out_ref.shape[1]
    query_part = out_ref.shape[0] // 8
    key_part = (joint_ref.shape[0] - out_ref.shape[0]) // 16
    lead = 2 * key_part + query_part
    key_from, value_from = 8 * query_part, 8 * (query_part + key_part)
    for k in range(8):
        e = jnp.bitwise_xor(place_ref[0], k)
        piece = pieces[k]
        joint_ref[pl.ds(pl.multiple_of(e * query_part, 16), query_part), :] = piece[:query_part]
        joint_ref[pl.ds(pl.multiple_of(key_from + e * key_part, 16), key_part), :] = piece[
            query_part : query_part + key_part
        ]
        joint_ref[pl.ds(pl.multiple_of(value_from + e * key_part, 16), key_part), :] = piece[
            query_part + key_part : lead
        ]
        out_ref[pl.ds(pl.multiple_of(e * query_part, 16), query_part), :] = piece[
            lead : lead + query_part
        ]
        vector_ref[e] = piece[lead + query_part :]


def assemble(pieces, query_part, key_part):
    width = pieces[0].shape[1]
    vector_rows = pieces[0].shape[0] - 2 * query_part - 2 * key_part
    whole = pl.BlockSpec(memory_space=pltpu.VMEM)
    return pl.pallas_call(
        assemble_kernel,
        out_shape=(
            jax.ShapeDtypeStruct((8 * (query_part + 2 * key_part), width), jnp.bfloat16),
            jax.ShapeDtypeStruct((8 * query_part, width), jnp.bfloat16),
            jax.ShapeDtypeStruct((8, vector_rows, width), jnp.bfloat16),
        ),
        in_specs=[pl.BlockSpec(memory_space=pltpu.SMEM)] + [whole] * 8,
        out_specs=(whole,) * 3,
        compiler_params=pltpu.CompilerParams(vmem_limit_bytes=KERNEL_BYTES),
        name="assemble",
    )(lax.axis_index("dp").reshape(1), *pieces)


def turn(rows, cosine, sine):
    half = HEAD_SIZE // 2
    first, second = rows[:half], rows[half:]
    return jnp.concatenate([first * cosine - second * sine, second * cosine + first * sine])


def project_kernel(x_ref, w_ref, q_bias_ref, v_bias_ref, cos_ref, sin_ref, q_ref, kv_ref):
    cosine, sine = cos_ref[...], sin_ref[...]
    joint = lax.dot_general(
        w_ref[...], x_ref[...], (((1,), (1,)), ((), ())), preferred_element_type=jnp.float32
    )
    for h in range(QUERY_HEADS):
        at = slice(h * HEAD_SIZE, (h + 1) * HEAD_SIZE)
        rows = turn(joint[at] + q_bias_ref[at], cosine, sine).astype(jnp.bfloat16)
        q_ref[at] = rows * jnp.bfloat16(HEAD_SIZE**-0.5)
    for g in range(KEY_VALUE_HEADS):
        at = slice(g * HEAD_SIZE, (g + 1) * HEAD_SIZE)
        first = (QUERY_HEADS + g) * HEAD_SIZE
        kv_ref[at] = turn(joint[first : first + HEAD_SIZE], cosine, sine).astype(jnp.bfloat16)
    key_width = KEY_VALUE_HEADS * HEAD_SIZE
    kv_ref[key_width:] = (
        joint[QUERY_HEADS * HEAD_SIZE + key_width :] + v_bias_ref[...]
    ).astype(jnp.bfloat16)


def project(normed, joint_t, query_bias, value_bias, cosine, sine):
    rows = normed.shape[0]
    whole = pl.BlockSpec(memory_space=pltpu.VMEM)
    query_width, key_width = QUERY_HEADS * HEAD_SIZE, KEY_VALUE_HEADS * HEAD_SIZE
    return pl.pallas_call(
        project_kernel,
        out_shape=(
            jax.ShapeDtypeStruct((query_width, rows), jnp.bfloat16),
            jax.ShapeDtypeStruct((2 * key_width, rows), jnp.bfloat16),
        ),
        in_specs=[whole] * 6,
        out_specs=(whole,) * 2,
        compiler_params=pltpu.CompilerParams(vmem_limit_bytes=KERNEL_BYTES),
        name="project",
    )(normed, joint_t, query_bias[:, None], value_bias[:, None], cosine, sine)


def feed_kernel(count, *refs):
    xs, ds = refs[:count], refs[count : 2 * count]
    gate_ref, up_ref, down_ref = refs[2 * count : 2 * count + 3]
    outs = refs[2 * count + 3 :]
    acts, d_gates, d_ups, d_xs, downs = [outs[i * count : (i + 1) * count] for i in range(5)]
    across = (((1,), (1,)), ((), ()))
    for k in range(count):
        x = xs[k][...]
        gate = jnp.dot(x, gate_ref[...], preferred_element_type=jnp.float32)
        up = jnp.dot(x, up_ref[...], preferred_element_type=jnp.float32)
        d_act = jnp.dot(ds[k][...], down_ref[...], preferred_element_type=jnp.float32)
        sigma = jax.nn.sigmoid(gate)
        silu = gate * sigma
        act = (silu * up).astype(jnp.bfloat16)
        d_gate = (d_act * up * sigma * (1.0 + gate * (1.0 - sigma))).astype(jnp.bfloat16)
        d_up = (d_act * silu).astype(jnp.bfloat16)
        acts[k][...] = act
        d_gates[k][...] = d_gate
        d_ups[k][...] = d_up
        d_x = lax.dot_general(d_gate, gate_ref[...], across, preferred_element_type=jnp.float32)
        d_x = d_x + lax.dot_general(
            d_up, up_ref[...], across, preferred_element_type=jnp.float32
        )
        d_xs[k][...] = d_x.astype(jnp.bfloat16)
        downs[k][...] = lax.dot_general(
            act, down_ref[...], across, preferred_element_type=jnp.float32
        ).astype(jnp.bfloat16)


def feed(xs, ds, gate_w, up_w, down_w):
    count = len(xs)
    rows, width = xs[0].shape
    hidden = gate_w.shape[1]
    whole = pl.BlockSpec(memory_space=pltpu.VMEM)
    narrow = jax.ShapeDtypeStruct((rows, hidden), jnp.bfloat16)
    wide = jax.ShapeDtypeStruct((rows, width), jnp.bfloat16)
    outs = pl.pallas_call(
        functools.partial(feed_kernel, count),
        out_shape=(narrow,) * (3 * count) + (wide,) * (2 * count),
        in_specs=[whole] * (2 * count + 3),
        out_specs=(whole,) * (5 * count),
        compiler_params=pltpu.CompilerParams(vmem_limit_bytes=KERNEL_BYTES),
        cost_estimate=pl.CostEstimate(
            flops=14 * count * rows * width * hidden,
            bytes_accessed=count * rows * (8 * width + 6 * hidden),
            transcendentals=count * rows * hidden,
        ),
        name="feed",
    )(*xs, *ds, gate_w, up_w, down_w)
    return [outs[i * count : (i + 1) * count] for i in range(5)]


def grad_kernel(count, *refs):
    lefts, rights, out_ref, total_ref = refs[:count], refs[count : 2 * count], refs[-2], refs[-1]
    for k in range(count):
        term = lax.dot_general(
            lefts[k][...],
            rights[k][...],
            (((0,), (0,)), ((), ())),
            preferred_element_type=jnp.float32,
        )
        if k == 0:
            total_ref[...] = term
        elif k < count - 1:
            total_ref[...] += term
        else:
            out_ref[...] = (total_ref[...] + term).astype(jnp.bfloat16)


def weight_grad(lefts, rights, size):
    if size != 8:
        return dot_tn(jnp.concatenate(lefts), jnp.concatenate(rights)).astype(jnp.bfloat16)
    rows, width = lefts[0].shape
    hidden = rights[0].shape[1]
    whole = pl.BlockSpec(memory_space=pltpu.VMEM)
    return pl.pallas_call(
        functools.partial(grad_kernel, size),
        out_shape=jax.ShapeDtypeStruct((width, hidden), jnp.bfloat16),
        in_specs=[whole] * (2 * size),
        out_specs=whole,
        scratch_shapes=[pltpu.VMEM((width, hidden), jnp.float32)],
        compiler_params=pltpu.CompilerParams(vmem_limit_bytes=KERNEL_BYTES),
        cost_estimate=pl.CostEstimate(
            flops=2 * size * rows * width * hidden,
            bytes_accessed=2 * size * rows * (width + hidden),
            transcendentals=0,
        ),
        name="weight_grad",
    )(*lefts, *rights)


def pick_rows(meta_ref, e, slots, kept):
    slot = lax.broadcasted_iota(jnp.int32, (slots, kept), 0)
    index = lax.broadcasted_iota(jnp.int32, (slots, kept), 1)
    chosen = (slot + meta_ref[1, e] == index) & (slot < meta_ref[0, e])
    return jnp.where(chosen, 1.0, 0.0).astype(jnp.bfloat16)


def range_bias(low_ref, high_ref, kept, rows):
    index = lax.broadcasted_iota(jnp.int32, (kept, rows), 0)
    inside = (index >= low_ref[...]) & (index <= high_ref[...])
    return jnp.where(inside, 0.0, NEGATIVE_FILL)


def attend_kernel(
    meta_ref, low_ref, high_ref, q_ref, kv_ref, o_ref, attn_ref, lse_ref, kvc_ref, bias_ref, k_ref
):
    shards, both, slots = kv_ref.shape
    kept, rows = bias_ref.shape
    head_groups = QUERY_HEADS // KEY_VALUE_HEADS
    key_width = both // 2
    packed = jnp.zeros((both, kept), jnp.float32)
    for e in range(shards):
        packed = packed + jnp.dot(
            kv_ref[e], pick_rows(meta_ref, e, slots, kept), preferred_element_type=jnp.float32
        )
    kvc_ref[...] = packed.astype(jnp.bfloat16)
    for g in range(KEY_VALUE_HEADS):
        k_ref[g] = packed[g * HEAD_SIZE : (g + 1) * HEAD_SIZE].T.astype(jnp.bfloat16)
    bias_ref[...] = range_bias(low_ref, high_ref, kept, rows)

    def pair(c, carry):
        found = []
        for j in range(2):
            h = 2 * c + j
            g = h // head_groups
            at = pl.multiple_of(h * HEAD_SIZE, HEAD_SIZE)
            s = jnp.dot(
                k_ref[g], q_ref[pl.ds(at, HEAD_SIZE), :], preferred_element_type=jnp.float32
            )
            s = s + bias_ref[...]
            top = jnp.max(s, 0, keepdims=True)
            p = jnp.exp(s - top)
            total = jnp.sum(p, 0, keepdims=True)
            v_at = pl.multiple_of(key_width + g * HEAD_SIZE, HEAD_SIZE)
            out = jnp.dot(
                kvc_ref[pl.ds(v_at, HEAD_SIZE), :],
                p.astype(jnp.bfloat16),
                preferred_element_type=jnp.float32,
            )
            out = out / total
            attn_ref[pl.ds(at, HEAD_SIZE), :] = out
            lse_ref[h] = top + jnp.log(total)
            found.append(out)
        block = jnp.concatenate(found, 0).T
        o_ref[:, pl.ds(pl.multiple_of(c * 2 * HEAD_SIZE, 2 * HEAD_SIZE), 2 * HEAD_SIZE)] = (
            block.astype(jnp.bfloat16)
        )
        return carry

    lax.fori_loop(0, QUERY_HEADS // 2, pair, 0)


def attend(meta, low, high, q, kv):
    shards, both, slots = kv.shape
    kept = shards * slots * 3 // 4
    width, rows = q.shape
    whole = pl.BlockSpec(memory_space=pltpu.VMEM)
    return pl.pallas_call(
        attend_kernel,
        out_shape=(
            jax.ShapeDtypeStruct((rows, width), jnp.bfloat16),
            jax.ShapeDtypeStruct((width, rows), jnp.float32),
            jax.ShapeDtypeStruct((QUERY_HEADS, 1, rows), jnp.float32),
            jax.ShapeDtypeStruct((both, kept), jnp.bfloat16),
        ),
        in_specs=[pl.BlockSpec(memory_space=pltpu.SMEM)] + [whole] * 4,
        out_specs=(whole,) * 4,
        scratch_shapes=[
            pltpu.VMEM((kept, rows), jnp.float32),
            pltpu.VMEM((KEY_VALUE_HEADS, kept, HEAD_SIZE), jnp.bfloat16),
        ],
        compiler_params=pltpu.CompilerParams(vmem_limit_bytes=ATTEND_BYTES),
        cost_estimate=pl.CostEstimate(
            flops=4 * width * rows * kept * 4,
            bytes_accessed=width * rows * 8,
            transcendentals=QUERY_HEADS * rows * kept,
        ),
        name="attend",
    )(meta, low, high, q, kv)


def attend_back_kernel(
    meta_ref,
    low_ref,
    high_ref,
    q_ref,
    kvc_ref,
    d_o_ref,
    attn_ref,
    lse_ref,
    cos_ref,
    sin_ref,
    d_q_ref,
    d_kv_ref,
    bias_ref,
    k_ref,
    v_ref,
    d_k_ref,
    d_v_ref,
):
    shards, both, slots = d_kv_ref.shape
    kept, rows = bias_ref.shape
    head_groups = QUERY_HEADS // KEY_VALUE_HEADS
    key_width = both // 2
    for g in range(KEY_VALUE_HEADS):
        k_ref[g] = kvc_ref[g * HEAD_SIZE : (g + 1) * HEAD_SIZE, :].astype(jnp.float32).T.astype(jnp.bfloat16)
        v_ref[g] = (
            kvc_ref[key_width + g * HEAD_SIZE : key_width + (g + 1) * HEAD_SIZE, :]
            .astype(jnp.float32)
            .T.astype(jnp.bfloat16)
        )
    bias_ref[...] = range_bias(low_ref, high_ref, kept, rows)
    d_k_ref[...] = jnp.zeros_like(d_k_ref)
    d_v_ref[...] = jnp.zeros_like(d_v_ref)

    def pair(c, carry):
        d_o_pair = d_o_ref[:, pl.ds(pl.multiple_of(c * 2 * HEAD_SIZE, 2 * HEAD_SIZE), 2 * HEAD_SIZE)]
        d_o_wide = d_o_pair.astype(jnp.float32).T
        pair_at = pl.multiple_of(c * 2 * HEAD_SIZE, 2 * HEAD_SIZE)
        q_rows = q_ref[pl.ds(pair_at, 2 * HEAD_SIZE), :].astype(jnp.float32).T.astype(jnp.bfloat16)
        for j in range(2):
            h = 2 * c + j
            g = h // head_groups
            at = pl.multiple_of(h * HEAD_SIZE, HEAD_SIZE)
            part = slice(j * HEAD_SIZE, (j + 1) * HEAD_SIZE)
            d_o_t = d_o_wide[part]
            delta = jnp.sum(d_o_t * attn_ref[pl.ds(at, HEAD_SIZE), :], 0, keepdims=True)
            s = jnp.dot(
                k_ref[g], q_ref[pl.ds(at, HEAD_SIZE), :], preferred_element_type=jnp.float32
            )
            p = jnp.exp(s + bias_ref[...] - lse_ref[h])
            d_p = jnp.dot(
                v_ref[g], d_o_t.astype(jnp.bfloat16), preferred_element_type=jnp.float32
            )
            d_s = (p * (d_p - delta)).astype(jnp.bfloat16)
            d_v_ref[g] += jnp.dot(
                p.astype(jnp.bfloat16), d_o_pair[:, part], preferred_element_type=jnp.float32
            )
            d_k_ref[g] += jnp.dot(d_s, q_rows[:, part], preferred_element_type=jnp.float32)
            k_at = pl.multiple_of(g * HEAD_SIZE, HEAD_SIZE)
            d_q = jnp.dot(
                kvc_ref[pl.ds(k_at, HEAD_SIZE), :], d_s, preferred_element_type=jnp.float32
            )
            d_q_ref[pl.ds(at, HEAD_SIZE), :] = turn(
                d_q * HEAD_SIZE**-0.5, cos_ref[...], -sin_ref[...]
            ).astype(jnp.bfloat16)
        return carry

    lax.fori_loop(0, QUERY_HEADS // 2, pair, 0)
    halves = [d_k_ref[g].T for g in range(KEY_VALUE_HEADS)]
    halves = halves + [d_v_ref[g].T for g in range(KEY_VALUE_HEADS)]
    packed = jnp.concatenate(halves, 0).astype(jnp.bfloat16)
    for e in range(shards):
        d_kv_ref[e] = lax.dot_general(
            packed,
            pick_rows(meta_ref, e, slots, kept),
            (((1,), (1,)), ((), ())),
            preferred_element_type=jnp.float32,
        ).astype(jnp.bfloat16)


def attend_back(meta, low, high, q, kvc, d_o, attn, lse, cosine, sine):
    both, kept = kvc.shape
    width, rows = q.shape
    shards = meta.shape[1]
    whole = pl.BlockSpec(memory_space=pltpu.VMEM)
    per_head = (KEY_VALUE_HEADS, kept, HEAD_SIZE)
    return pl.pallas_call(
        attend_back_kernel,
        out_shape=(
            jax.ShapeDtypeStruct((width, rows), jnp.bfloat16),
            jax.ShapeDtypeStruct((shards, both, rows), jnp.bfloat16),
        ),
        in_specs=[pl.BlockSpec(memory_space=pltpu.SMEM)] + [whole] * 9,
        out_specs=(whole,) * 2,
        scratch_shapes=[
            pltpu.VMEM((kept, rows), jnp.float32),
            pltpu.VMEM(per_head, jnp.bfloat16),
            pltpu.VMEM(per_head, jnp.bfloat16),
            pltpu.VMEM(per_head, jnp.float32),
            pltpu.VMEM(per_head, jnp.float32),
        ],
        compiler_params=pltpu.CompilerParams(vmem_limit_bytes=ATTEND_BYTES),
        cost_estimate=pl.CostEstimate(
            flops=10 * width * rows * kept * 4,
            bytes_accessed=width * rows * 12,
            transcendentals=QUERY_HEADS * rows * kept,
        ),
        name="attend_back",
    )(meta, low, high, q, kvc, d_o, attn, lse, cosine, sine)


def body(
    tokens,
    cotangent,
    counts,
    lengths,
    attn_gain,
    w_query,
    b_query,
    w_key,
    w_value,
    b_value,
    w_out,
    mlp_gain,
    w_gate,
    w_up,
    w_down,
):
    lanes = lax.axis_size("dp")
    fsdp_size = lax.axis_size("fsdp")
    token_rows, width = tokens.shape[1:]
    inputs = tokens[0].astype(jnp.float32)
    valid, position, low, high, meta = own_slots(
        counts[0], lengths[0], lax.axis_index("fsdp"), token_rows
    )
    valid_col = valid.astype(jnp.float32)[:, None]
    query_part, key_part, out_part = w_query.shape[1], w_key.shape[1], w_out.shape[1]
    hidden_part = w_gate.shape[1]
    pieces_each = lanes // fsdp_size
    query_width, key_width = QUERY_HEADS * HEAD_SIZE, KEY_VALUE_HEADS * HEAD_SIZE
    rows_each = w_gate.shape[0]

    projections = (
        gather_rows(jnp.concatenate([w_query, w_key, w_value, w_out], 1), fsdp_size)
        .reshape(width, -1)
        .T
    )
    joint_rows = projections.shape[0]
    vector_row = jnp.concatenate([attn_gain, b_query, b_value, mlp_gain])
    vector_count = vector_row.shape[0]
    vector_block = jnp.zeros((16, width), jnp.bfloat16).at[0, :vector_count].set(vector_row)
    own_block = jnp.concatenate([projections, vector_block])
    blocks = run(gather_steps(own_block, lanes))
    down_t = w_down.T.reshape(out_part, pieces_each, hidden_part).transpose(1, 0, 2)
    down_t, projections = lax.optimization_barrier((down_t, projections))
    down_slabs = lax.all_gather(down_t.reshape(-1, hidden_part), "fsdp", axis=0)
    pair_own, down_slabs = lax.optimization_barrier(
        (jnp.concatenate([w_gate, w_up]), down_slabs)
    )
    pair_slabs = lax.all_gather(pair_own, "fsdp", axis=0)
    gate_w = pair_slabs[:, :rows_each].reshape(width, hidden_part)
    up_w = pair_slabs[:, rows_each:].reshape(width, hidden_part)
    grad_out = cotangent[0].astype(jnp.float32)
    d_down = (valid_col * grad_out).astype(jnp.bfloat16)
    d_down, blocks = lax.optimization_barrier((d_down, blocks))
    d_down_moves = gather_steps(d_down, lanes)
    d_down_near, _ = next(d_down_moves)
    down_moves = exchange_steps(down_slabs.reshape(lanes, out_part, hidden_part), lanes)
    down_near, _ = next(down_moves)

    edges = (0, query_part, query_part + key_part, query_part + 2 * key_part, joint_rows)
    if lanes == 8:
        joint_t, wo_t, vector_table = assemble(blocks, query_part, key_part)
        vector_table = vector_table[:, 0, :vector_count].astype(jnp.float32)
    else:
        spread = jnp.stack(blocks)
        joint_t = jnp.concatenate(
            [spread[:, edges[i] : edges[i + 1]].reshape(-1, width) for i in range(3)]
        )
        wo_t = spread[:, edges[3] : edges[4]].reshape(-1, width)
        vector_table = spread[:, joint_rows, :vector_count].astype(jnp.float32)
    marks = [0]
    for size in (query_part, query_part, key_part, query_part):
        marks.append(marks[-1] + size)
    gain_one, query_bias, value_bias, gain_two = [
        vector_table[:, marks[i] : marks[i + 1]].reshape(-1) for i in range(4)
    ]

    inv_one = lax.rsqrt(jnp.mean(inputs * inputs, -1, keepdims=True) + EPS)
    unit_one = inputs * inv_one
    normed = (unit_one * gain_one).astype(jnp.bfloat16)
    cosine, sine = rope_tables(position.astype(jnp.float32), HEAD_SIZE // 2)
    query_rows, pair_rows = project(normed, joint_t, query_bias, value_bias, cosine, sine)
    d_down_near, pair_rows = tie(d_down_near, pair_rows)
    d_down_far, _ = d_down_moves.send(d_down_near)
    gathered = gather_rows(pair_rows, fsdp_size)
    (d_down_far, down_near), gathered = tie((d_down_far, down_near), gathered)
    d_down_pieces = finish(d_down_moves, d_down_far)
    down_far, _ = down_moves.send(down_near)
    heads_out, attention, log_total, packed_kv = attend(
        meta, low[None], high[None], query_rows, gathered
    )
    down_far, heads_out = tie(down_far, heads_out)
    down_w = finish(down_moves, down_far).reshape(width, hidden_part)
    proj = dot_nt(heads_out, wo_t)
    hidden = inputs + valid_col * proj
    inv_two = lax.rsqrt(jnp.mean(hidden * hidden, -1, keepdims=True) + EPS)
    unit_two = hidden * inv_two
    normed2 = (unit_two * gain_two).astype(jnp.bfloat16)

    normed2, down_w = tie(normed2, down_w)
    results = [[], [], [], [], []]

    def feed_more(pieces, cotangents):
        for first in range(0, len(pieces), 2):
            piece = slice(first, first + 2)
            found = feed(pieces[piece], cotangents[piece], gate_w, up_w, down_w)
            for group, values in zip(results, found):
                group.extend(values)

    moves = gather_steps(normed2, lanes)
    near, ready = next(moves)
    feed_more(ready, d_down_pieces[:2])
    near, results = tie(near, results)
    far, ready = moves.send(near)
    feed_more(ready, d_down_pieces[2 : lanes - 2])
    far, results = tie(far, results)
    normed2_pieces = finish(moves, far)
    feed_more(normed2_pieces[lanes - 2 :], d_down_pieces[lanes - 2 :])
    acts, d_gates, d_ups, d_n2_parts, down_parts = results
    grad_down = weight_grad(d_down_pieces, acts, lanes)
    grad_gate = weight_grad(normed2_pieces, d_gates, lanes)
    grad_up = weight_grad(normed2_pieces, d_ups, lanes)
    moves = scatter_steps(d_n2_parts, lanes)
    far, _ = next(moves)
    far, grad_down = tie(far, grad_down)
    near, _ = moves.send(far)
    near, (grad_gate, grad_up) = tie(near, (grad_gate, grad_up))
    d_n2 = finish(moves, near)
    (down_parts, grad_down), d_n2 = tie((down_parts, grad_down), d_n2)
    down_moves = scatter_steps(down_parts, lanes)
    down_far, _ = next(down_moves)
    grad_moves = exchange_steps(grad_down.reshape(lanes, out_part, hidden_part), lanes)
    grad_near, _ = next(grad_moves)
    pair_grads = jnp.concatenate(
        [
            grad_gate.reshape(fsdp_size, rows_each, hidden_part),
            grad_up.reshape(fsdp_size, rows_each, hidden_part),
        ],
        1,
    )

    scaled_two = d_n2 * gain_two
    dh = grad_out + inv_two * (
        scaled_two - unit_two * jnp.mean(scaled_two * unit_two, -1, keepdims=True)
    )
    grad_gain_two = jnp.sum(d_n2 * unit_two, 0)
    d_proj = (valid_col * dh).astype(jnp.bfloat16)
    pair_sums = lax.psum_scatter(
        pair_grads, "fsdp", scatter_dimension=0, tiled=False
    ).astype(jnp.float32)
    grad_w_gate = pair_sums[:rows_each]
    grad_w_up = pair_sums[rows_each:]
    out_grad = lax.psum_scatter(
        dot_tn(d_proj, heads_out).astype(jnp.bfloat16).reshape(lanes, out_part, -1),
        "dp",
        scatter_dimension=0,
        tiled=False,
    )
    head_gradient = dot_nn(d_proj, wo_t).astype(jnp.bfloat16)
    grad_near, head_gradient = tie(grad_near, head_gradient)
    grad_far, _ = grad_moves.send(grad_near)
    d_q_pre, d_kv = attend_back(
        meta,
        low[None],
        high[None],
        query_rows,
        packed_kv,
        head_gradient,
        attention,
        log_total,
        cosine,
        sine,
    )
    (grad_far, down_far), d_kv = tie((grad_far, down_far), d_kv)
    grad_down = finish(grad_moves, grad_far)
    down_near, _ = down_moves.send(down_far)
    own_kv = scatter_rows(d_kv, fsdp_size)
    down_near, own_kv = tie(down_near, own_kv)
    down = finish(down_moves, down_near)
    mixed = (hidden + valid_col * down).astype(jnp.bfloat16)
    grad_w_down = (
        lax.psum_scatter(
            grad_down.reshape(fsdp_size, rows_each, hidden_part),
            "fsdp",
            scatter_dimension=0,
            tiled=False,
        )
        .astype(jnp.float32)
        .reshape(pieces_each, out_part, hidden_part)
        .transpose(0, 2, 1)
        .reshape(-1, out_part)
    )
    d_k_pre = rotary_reverse(own_kv[:key_width], cosine, sine).astype(jnp.bfloat16)
    d_v_pre = own_kv[key_width:].astype(jnp.bfloat16)
    d_joint = jnp.concatenate([d_q_pre, d_k_pre, d_v_pre])
    d_n1 = dot_tn(d_joint, joint_t)
    scaled_one = d_n1 * gain_one
    d_tokens = (
        dh + inv_one * (scaled_one - unit_one * jnp.mean(scaled_one * unit_one, -1, keepdims=True))
    ).astype(jnp.bfloat16)
    local_vectors = (
        jnp.sum(d_n1 * unit_one, 0),
        jnp.sum(d_q_pre.astype(jnp.float32), 1),
        jnp.sum(d_v_pre.astype(jnp.float32), 1),
        grad_gain_two,
    )
    vector_rows = jnp.concatenate([v.reshape(lanes, -1) for v in local_vectors], 1)
    vector_rows = jnp.pad(vector_rows, ((0, 0), (0, width - vector_count)))
    vector_rows = jnp.pad(vector_rows[:, None].astype(jnp.bfloat16), ((0, 0), (0, 15), (0, 0)))
    joint_grads = dot_nn(d_joint, normed).astype(jnp.bfloat16)
    joint_parts = jnp.concatenate(
        [
            joint_grads[:query_width].reshape(lanes, query_part, width),
            joint_grads[query_width : query_width + key_width].reshape(lanes, key_part, width),
            joint_grads[query_width + key_width :].reshape(lanes, key_part, width),
            vector_rows,
        ],
        1,
    )
    joint_sum = run(scatter_steps([joint_parts[e] for e in range(lanes)], lanes, ordered=True))
    qkv_rows = query_part + 2 * key_part
    row_sums = scatter_rows(
        jnp.concatenate([joint_sum[:qkv_rows].astype(jnp.bfloat16), out_grad])
        .T.reshape(fsdp_size, rows_each, joint_rows),
        fsdp_size,
    )
    grad_w_query, grad_w_key, grad_w_value, out_grad = [
        row_sums[:, edges[i] : edges[i + 1]] for i in range(4)
    ]
    own_vectors = joint_sum[qkv_rows, :vector_count]
    vector_sum = own_vectors
    for k in range(1, fsdp_size):
        vector_sum = vector_sum + lax.ppermute(
            own_vectors, "fsdp", [(i, (i + k) % fsdp_size) for i in range(fsdp_size)]
        )
    vector_pieces = [vector_sum[marks[i] : marks[i + 1]] for i in range(4)]
    return (
        mixed[None],
        d_tokens[None],
        vector_pieces[0],
        grad_w_query,
        vector_pieces[1],
        grad_w_key,
        grad_w_value,
        vector_pieces[2],
        out_grad,
        vector_pieces[3],
        grad_w_gate,
        grad_w_up,
        grad_w_down,
    )


def solution(mesh):
    placed = (
        P("dp", "fsdp", None),
        P("dp", "fsdp", None),
        P("dp", None),
        P("dp", None),
        P("dp"),
        P("fsdp", "dp"),
        P("dp"),
        P("fsdp", "dp"),
        P("fsdp", "dp"),
        P("dp"),
        P("fsdp", "dp"),
        P("dp"),
        P("fsdp", "dp"),
        P("fsdp", "dp"),
        P("fsdp", "dp"),
    )
    return jax.shard_map(
        body,
        mesh=mesh,
        in_specs=placed,
        out_specs=(
            P("dp", "fsdp", None),
            P("dp", "fsdp", None),
            P("dp"),
            P("fsdp", "dp"),
            P("dp"),
            P("fsdp", "dp"),
            P("fsdp", "dp"),
            P("dp"),
            P("fsdp", "dp"),
            P("dp"),
            P("fsdp", "dp"),
            P("fsdp", "dp"),
            P("fsdp", "dp"),
        ),
        check_vma=False,
    )
```

```python
import functools

import jax
import jax.numpy as jnp
from jax import lax
from jax.experimental import pallas as pl
from jax.experimental.pallas import tpu as pltpu
from jax.sharding import PartitionSpec as P

QUERY_HEADS = 14
KEY_VALUE_HEADS = 2
HEAD_SIZE = 64
KERNEL_BYTES = 24 * 2**20
ATTEND_BYTES = 32 * 2**20


EPS = 1e-06
THETA = 1000000.0
NEGATIVE_FILL = -1e30


def own_slots(count_row, length_row, place, slots):
    before = jnp.cumsum(count_row) - count_row
    inner = jnp.arange(slots, dtype=jnp.int32)
    valid = inner < count_row[place]
    index = before[place] + inner
    ends = jnp.cumsum(length_row)
    numbers = jnp.sum((index[:, None] >= ends[None, :]).astype(jnp.int32), 1)
    starts = ends - length_row
    owners = jnp.arange(length_row.shape[0], dtype=jnp.int32)
    start_of = jnp.sum(
        (numbers[:, None] == owners[None, :]).astype(jnp.int32) * starts[None, :], 1
    )
    position = jnp.where(valid, index - start_of, 0)
    opened = jnp.max(jnp.where(index[:, None] >= ends[None, :], ends[None, :], 0), 1)
    low = jnp.where(valid, opened, 0)
    high = jnp.where(valid, index, 0)
    return valid, position, low, high, jnp.stack([count_row, before])


def rope_tables(position, half):
    steps = jnp.arange(half, dtype=jnp.float32) * (1.0 / half)
    freq = THETA ** (-steps)
    angle = freq[:, None] * position[None, :]
    return jnp.cos(angle), jnp.sin(angle)


def rotary_apply(rows, cosine, sine):
    cube = rows.reshape(-1, 2, HEAD_SIZE // 2, rows.shape[1])
    first, second = cube[:, 0], cube[:, 1]
    turned = [first * cosine - second * sine, second * cosine + first * sine]
    return jnp.stack(turned, 1).reshape(rows.shape)


def rotary_reverse(rows, cosine, sine):
    return rotary_apply(rows, cosine, -sine)


def flip(array, mask, size):
    return lax.ppermute(array, "dp", [(i, i ^ mask) for i in range(size)])


def tie(first, second):
    return lax.optimization_barrier((first, second))


def finish(steps, pending):
    try:
        steps.send(pending)
    except StopIteration as end:
        return end.value


def run(steps):
    try:
        pending = next(steps)
        while True:
            pending = steps.send(pending[0])
    except StopIteration as end:
        return end.value


def gather_steps(rows, size):
    if size != 8:
        whole = lax.all_gather(rows, "dp", axis=0)
        pieces = [whole[k] for k in range(size)]
        yield (), pieces[:2]
        yield (), pieces[2 : size - 2]
        return pieces
    half = rows.shape[0] // 2
    by_x, by_y, by_core = flip(rows, 2, 8), flip(rows, 4, 8), flip(rows, 1, 8)
    by_x, by_y = yield (by_x, by_y), [rows, by_core]
    far_a, far_b = flip(by_x[:half], 4, 8), flip(by_y[half:], 2, 8)
    core_x, core_y = flip(by_x, 1, 8), flip(by_y, 1, 8)
    far_a, far_b = yield (far_a, far_b), [by_x, core_x, by_y, core_y]
    far = jnp.concatenate([far_a, far_b])
    return [rows, by_core, by_x, core_x, by_y, core_y, far, flip(far, 1, 8)]


def scatter_steps(parts, size, ordered=False):
    if size != 8:
        total = lax.psum_scatter(jnp.stack(parts), "dp", scatter_dimension=0, tiled=False)
        yield (), None
        yield (), None
        return total.astype(jnp.float32)
    if ordered:
        place = lax.axis_index("dp")
        parts = jnp.stack(parts)
        parts = [lax.dynamic_index_in_dim(parts, place ^ k, 0, False) for k in range(8)]
    half = parts[0].shape[0] // 2
    wide = jnp.float32
    seven, five, three, one = [flip(parts[k], 1, 8) for k in (7, 5, 3, 1)]
    far = (parts[6].astype(wide) + seven.astype(wide)).astype(jnp.bfloat16)
    far_x, far_y = yield (flip(far[:half], 2, 8), flip(far[half:], 4, 8)), None
    on_y = parts[4].astype(wide) + five.astype(wide)
    on_x = parts[2].astype(wide) + three.astype(wide)
    on_y = jnp.concatenate([on_y[:half] + far_x.astype(wide), on_y[half:]]).astype(jnp.bfloat16)
    on_x = jnp.concatenate([on_x[:half], on_x[half:] + far_y.astype(wide)]).astype(jnp.bfloat16)
    got_x, got_y = yield (flip(on_x, 2, 8), flip(on_y, 4, 8)), None
    own = parts[0].astype(wide) + one.astype(wide)
    return own + got_x.astype(wide) + got_y.astype(wide)


def exchange_steps(parts, size):
    if size != 8:
        result = lax.all_to_all(parts, "dp", 0, 0, tiled=True)
        yield (), None
        return result
    place = lax.axis_index("dp")
    chip, core = place // 2, place % 2
    block = parts.reshape((4, 2) + parts.shape[1:])
    kept = lax.dynamic_index_in_dim(block, core, 1, True)
    got = flip(lax.dynamic_index_in_dim(block, 1 - core, 1, True), 1, 8)
    block = jnp.where(
        core == 0, jnp.concatenate([kept, got], 1), jnp.concatenate([got, kept], 1)
    )
    moved = tuple(
        flip(lax.dynamic_index_in_dim(block, chip ^ k, 0, True), 2 * k, 8) for k in (1, 2, 3)
    )
    moved = yield moved, None
    for k in (1, 2, 3):
        block = lax.dynamic_update_slice_in_dim(block, moved[k - 1], chip ^ k, 0)
    return block.reshape(parts.shape)


def gather_rows(rows, size):
    place = lax.axis_index("fsdp")
    result = jnp.zeros((size,) + rows.shape, rows.dtype)
    result = lax.dynamic_update_slice_in_dim(result, rows[None], place, 0)
    for k in range(1, size):
        piece = lax.ppermute(rows, "fsdp", [(i, (i + k) % size) for i in range(size)])
        result = lax.dynamic_update_slice_in_dim(result, piece[None], (place + size - k) % size, 0)
    return result


def scatter_rows(parts, size):
    place = lax.axis_index("fsdp")
    sent = parts.astype(jnp.bfloat16)
    total = lax.dynamic_index_in_dim(parts, place, 0, False).astype(jnp.float32)
    for k in range(1, size):
        piece = lax.dynamic_index_in_dim(sent, (place + k) % size, 0, False)
        total = total + lax.ppermute(
            piece, "fsdp", [(i, (i + k) % size) for i in range(size)]
        ).astype(jnp.float32)
    return total


def gather_earlier(rows, size):
    place = lax.axis_index("fsdp")
    result = jnp.zeros((size,) + rows.shape, rows.dtype)
    result = lax.dynamic_update_slice_in_dim(result, rows[None], place, 0)
    for k in range(1, size):
        piece = lax.ppermute(rows, "fsdp", [(i, i + k) for i in range(size - k)])
        result = lax.dynamic_update_slice_in_dim(result, piece[None], (place + size - k) % size, 0)
    return result


def scatter_earlier(parts, size):
    place = lax.axis_index("fsdp")
    total = lax.dynamic_index_in_dim(parts, place, 0, False).astype(jnp.float32)
    for k in range(1, size):
        piece = lax.dynamic_index_in_dim(parts, (place + size - k) % size, 0, False)
        total = total + lax.ppermute(
            piece, "fsdp", [(i, i - k) for i in range(k, size)]
        ).astype(jnp.float32)
    return total


def dot_tn(left, right):
    return lax.dot_general(
        left, right, (((0,), (0,)), ((), ())), preferred_element_type=jnp.float32
    )


def dot_nt(left, right):
    return lax.dot_general(
        left, right, (((1,), (1,)), ((), ())), preferred_element_type=jnp.float32
    )


def dot_nn(left, right):
    return jnp.dot(left, right, preferred_element_type=jnp.float32)


def assemble_kernel(place_ref, *refs):
    pieces, (joint_ref, out_ref, vector_ref) = refs[:8], refs[8:]
    width = out_ref.shape[1]
    query_part = out_ref.shape[0] // 8
    key_part = (joint_ref.shape[0] - out_ref.shape[0]) // 16
    lead = 2 * key_part + query_part
    key_from, value_from = 8 * query_part, 8 * (query_part + key_part)
    for k in range(8):
        e = jnp.bitwise_xor(place_ref[0], k)
        piece = pieces[k]
        joint_ref[pl.ds(pl.multiple_of(e * query_part, 16), query_part), :] = piece[:query_part]
        joint_ref[pl.ds(pl.multiple_of(key_from + e * key_part, 16), key_part), :] = piece[
            query_part : query_part + key_part
        ]
        joint_ref[pl.ds(pl.multiple_of(value_from + e * key_part, 16), key_part), :] = piece[
            query_part + key_part : lead
        ]
        out_ref[pl.ds(pl.multiple_of(e * query_part, 16), query_part), :] = piece[
            lead : lead + query_part
        ]
        vector_ref[e] = piece[lead + query_part :]


def assemble(pieces, query_part, key_part):
    width = pieces[0].shape[1]
    vector_rows = pieces[0].shape[0] - 2 * query_part - 2 * key_part
    whole = pl.BlockSpec(memory_space=pltpu.VMEM)
    return pl.pallas_call(
        assemble_kernel,
        out_shape=(
            jax.ShapeDtypeStruct((8 * (query_part + 2 * key_part), width), jnp.bfloat16),
            jax.ShapeDtypeStruct((8 * query_part, width), jnp.bfloat16),
            jax.ShapeDtypeStruct((8, vector_rows, width), jnp.bfloat16),
        ),
        in_specs=[pl.BlockSpec(memory_space=pltpu.SMEM)] + [whole] * 8,
        out_specs=(whole,) * 3,
        compiler_params=pltpu.CompilerParams(vmem_limit_bytes=KERNEL_BYTES),
        name="assemble",
    )(lax.axis_index("dp").reshape(1), *pieces)


def turn(rows, cosine, sine):
    half = HEAD_SIZE // 2
    first, second = rows[:half], rows[half:]
    return jnp.concatenate([first * cosine - second * sine, second * cosine + first * sine])


def project_kernel(x_ref, w_ref, q_bias_ref, v_bias_ref, cos_ref, sin_ref, q_ref, kv_ref):
    cosine, sine = cos_ref[...], sin_ref[...]
    joint = lax.dot_general(
        w_ref[...], x_ref[...], (((1,), (1,)), ((), ())), preferred_element_type=jnp.float32
    )
    for h in range(QUERY_HEADS):
        at = slice(h * HEAD_SIZE, (h + 1) * HEAD_SIZE)
        rows = turn(joint[at] + q_bias_ref[at], cosine, sine).astype(jnp.bfloat16)
        q_ref[at] = rows * jnp.bfloat16(HEAD_SIZE**-0.5)
    for g in range(KEY_VALUE_HEADS):
        at = slice(g * HEAD_SIZE, (g + 1) * HEAD_SIZE)
        first = (QUERY_HEADS + g) * HEAD_SIZE
        kv_ref[at] = turn(joint[first : first + HEAD_SIZE], cosine, sine).astype(jnp.bfloat16)
    key_width = KEY_VALUE_HEADS * HEAD_SIZE
    kv_ref[key_width:] = (
        joint[QUERY_HEADS * HEAD_SIZE + key_width :] + v_bias_ref[...]
    ).astype(jnp.bfloat16)


def project(normed, joint_t, query_bias, value_bias, cosine, sine):
    rows = normed.shape[0]
    whole = pl.BlockSpec(memory_space=pltpu.VMEM)
    query_width, key_width = QUERY_HEADS * HEAD_SIZE, KEY_VALUE_HEADS * HEAD_SIZE
    return pl.pallas_call(
        project_kernel,
        out_shape=(
            jax.ShapeDtypeStruct((query_width, rows), jnp.bfloat16),
            jax.ShapeDtypeStruct((2 * key_width, rows), jnp.bfloat16),
        ),
        in_specs=[whole] * 6,
        out_specs=(whole,) * 2,
        compiler_params=pltpu.CompilerParams(vmem_limit_bytes=KERNEL_BYTES),
        name="project",
    )(normed, joint_t, query_bias[:, None], value_bias[:, None], cosine, sine)


def feed_kernel(count, *refs):
    xs, ds = refs[:count], refs[count : 2 * count]
    gate_ref, up_ref, down_ref = refs[2 * count : 2 * count + 3]
    outs = refs[2 * count + 3 :]
    acts, d_gates, d_ups, d_xs, downs = [outs[i * count : (i + 1) * count] for i in range(5)]
    across = (((1,), (1,)), ((), ()))
    for k in range(count):
        x = xs[k][...]
        gate = jnp.dot(x, gate_ref[...], preferred_element_type=jnp.float32)
        up = jnp.dot(x, up_ref[...], preferred_element_type=jnp.float32)
        d_act = jnp.dot(ds[k][...], down_ref[...], preferred_element_type=jnp.float32)
        sigma = jax.nn.sigmoid(gate)
        silu = gate * sigma
        act = (silu * up).astype(jnp.bfloat16)
        d_gate = (d_act * up * sigma * (1.0 + gate * (1.0 - sigma))).astype(jnp.bfloat16)
        d_up = (d_act * silu).astype(jnp.bfloat16)
        acts[k][...] = act
        d_gates[k][...] = d_gate
        d_ups[k][...] = d_up
        d_x = lax.dot_general(d_gate, gate_ref[...], across, preferred_element_type=jnp.float32)
        d_x = d_x + lax.dot_general(
            d_up, up_ref[...], across, preferred_element_type=jnp.float32
        )
        d_xs[k][...] = d_x.astype(jnp.bfloat16)
        downs[k][...] = lax.dot_general(
            act, down_ref[...], across, preferred_element_type=jnp.float32
        ).astype(jnp.bfloat16)


def feed(xs, ds, gate_w, up_w, down_w):
    count = len(xs)
    rows, width = xs[0].shape
    hidden = gate_w.shape[1]
    whole = pl.BlockSpec(memory_space=pltpu.VMEM)
    narrow = jax.ShapeDtypeStruct((rows, hidden), jnp.bfloat16)
    wide = jax.ShapeDtypeStruct((rows, width), jnp.bfloat16)
    outs = pl.pallas_call(
        functools.partial(feed_kernel, count),
        out_shape=(narrow,) * (3 * count) + (wide,) * (2 * count),
        in_specs=[whole] * (2 * count + 3),
        out_specs=(whole,) * (5 * count),
        compiler_params=pltpu.CompilerParams(vmem_limit_bytes=KERNEL_BYTES),
        cost_estimate=pl.CostEstimate(
            flops=14 * count * rows * width * hidden,
            bytes_accessed=count * rows * (8 * width + 6 * hidden),
            transcendentals=count * rows * hidden,
        ),
        name="feed",
    )(*xs, *ds, gate_w, up_w, down_w)
    return [outs[i * count : (i + 1) * count] for i in range(5)]


def grad_kernel(count, *refs):
    lefts, rights, out_ref, total_ref = refs[:count], refs[count : 2 * count], refs[-2], refs[-1]
    for k in range(count):
        term = lax.dot_general(
            lefts[k][...],
            rights[k][...],
            (((0,), (0,)), ((), ())),
            preferred_element_type=jnp.float32,
        )
        if k == 0:
            total_ref[...] = term
        elif k < count - 1:
            total_ref[...] += term
        else:
            out_ref[...] = (total_ref[...] + term).astype(jnp.bfloat16)


def weight_grad(lefts, rights, size):
    if size != 8:
        return dot_tn(jnp.concatenate(lefts), jnp.concatenate(rights)).astype(jnp.bfloat16)
    rows, width = lefts[0].shape
    hidden = rights[0].shape[1]
    whole = pl.BlockSpec(memory_space=pltpu.VMEM)
    return pl.pallas_call(
        functools.partial(grad_kernel, size),
        out_shape=jax.ShapeDtypeStruct((width, hidden), jnp.bfloat16),
        in_specs=[whole] * (2 * size),
        out_specs=whole,
        scratch_shapes=[pltpu.VMEM((width, hidden), jnp.float32)],
        compiler_params=pltpu.CompilerParams(vmem_limit_bytes=KERNEL_BYTES),
        cost_estimate=pl.CostEstimate(
            flops=2 * size * rows * width * hidden,
            bytes_accessed=2 * size * rows * (width + hidden),
            transcendentals=0,
        ),
        name="weight_grad",
    )(*lefts, *rights)


def pick_rows(meta_ref, e, slots, kept):
    slot = lax.broadcasted_iota(jnp.int32, (slots, kept), 0)
    index = lax.broadcasted_iota(jnp.int32, (slots, kept), 1)
    chosen = (slot + meta_ref[1, e] == index) & (slot < meta_ref[0, e])
    return jnp.where(chosen, 1.0, 0.0).astype(jnp.bfloat16)


def range_bias(low_ref, high_ref, kept, rows):
    index = lax.broadcasted_iota(jnp.int32, (kept, rows), 0)
    inside = (index >= low_ref[...]) & (index <= high_ref[...])
    return jnp.where(inside, 0.0, NEGATIVE_FILL)


def attend_kernel(
    meta_ref, low_ref, high_ref, q_ref, kv_ref, o_ref, attn_ref, lse_ref, kvc_ref, bias_ref, k_ref
):
    shards, both, slots = kv_ref.shape
    kept, rows = bias_ref.shape
    head_groups = QUERY_HEADS // KEY_VALUE_HEADS
    key_width = both // 2
    packed = jnp.zeros((both, kept), jnp.float32)
    for e in range(shards):
        packed = packed + jnp.dot(
            kv_ref[e], pick_rows(meta_ref, e, slots, kept), preferred_element_type=jnp.float32
        )
    kvc_ref[...] = packed.astype(jnp.bfloat16)
    for g in range(KEY_VALUE_HEADS):
        k_ref[g] = packed[g * HEAD_SIZE : (g + 1) * HEAD_SIZE].T.astype(jnp.bfloat16)
    bias_ref[...] = range_bias(low_ref, high_ref, kept, rows)

    def pair(c, carry):
        found = []
        for j in range(2):
            h = 2 * c + j
            g = h // head_groups
            at = pl.multiple_of(h * HEAD_SIZE, HEAD_SIZE)
            s = jnp.dot(
                k_ref[g], q_ref[pl.ds(at, HEAD_SIZE), :], preferred_element_type=jnp.float32
            )
            s = s + bias_ref[...]
            top = jnp.max(s, 0, keepdims=True)
            p = jnp.exp(s - top)
            total = jnp.sum(p, 0, keepdims=True)
            v_at = pl.multiple_of(key_width + g * HEAD_SIZE, HEAD_SIZE)
            out = jnp.dot(
                kvc_ref[pl.ds(v_at, HEAD_SIZE), :],
                p.astype(jnp.bfloat16),
                preferred_element_type=jnp.float32,
            )
            out = out / total
            attn_ref[pl.ds(at, HEAD_SIZE), :] = out
            lse_ref[h] = top + jnp.log(total)
            found.append(out)
        block = jnp.concatenate(found, 0).T
        o_ref[:, pl.ds(pl.multiple_of(c * 2 * HEAD_SIZE, 2 * HEAD_SIZE), 2 * HEAD_SIZE)] = (
            block.astype(jnp.bfloat16)
        )
        return carry

    lax.fori_loop(0, QUERY_HEADS // 2, pair, 0)


def attend(meta, low, high, q, kv):
    shards, both, slots = kv.shape
    kept = shards * slots * 3 // 4
    width, rows = q.shape
    whole = pl.BlockSpec(memory_space=pltpu.VMEM)
    return pl.pallas_call(
        attend_kernel,
        out_shape=(
            jax.ShapeDtypeStruct((rows, width), jnp.bfloat16),
            jax.ShapeDtypeStruct((width, rows), jnp.float32),
            jax.ShapeDtypeStruct((QUERY_HEADS, 1, rows), jnp.float32),
            jax.ShapeDtypeStruct((both, kept), jnp.bfloat16),
        ),
        in_specs=[pl.BlockSpec(memory_space=pltpu.SMEM)] + [whole] * 4,
        out_specs=(whole,) * 4,
        scratch_shapes=[
            pltpu.VMEM((kept, rows), jnp.float32),
            pltpu.VMEM((KEY_VALUE_HEADS, kept, HEAD_SIZE), jnp.bfloat16),
        ],
        compiler_params=pltpu.CompilerParams(vmem_limit_bytes=ATTEND_BYTES),
        cost_estimate=pl.CostEstimate(
            flops=4 * width * rows * kept * 4,
            bytes_accessed=width * rows * 8,
            transcendentals=QUERY_HEADS * rows * kept,
        ),
        name="attend",
    )(meta, low, high, q, kv)


def attend_back_kernel(
    meta_ref,
    low_ref,
    high_ref,
    q_ref,
    kvc_ref,
    d_o_ref,
    attn_ref,
    lse_ref,
    cos_ref,
    sin_ref,
    d_q_ref,
    d_kv_ref,
    bias_ref,
    k_ref,
    v_ref,
    d_k_ref,
    d_v_ref,
):
    shards, both, slots = d_kv_ref.shape
    kept, rows = bias_ref.shape
    head_groups = QUERY_HEADS // KEY_VALUE_HEADS
    key_width = both // 2
    for g in range(KEY_VALUE_HEADS):
        k_ref[g] = kvc_ref[g * HEAD_SIZE : (g + 1) * HEAD_SIZE, :].astype(jnp.float32).T.astype(jnp.bfloat16)
        v_ref[g] = (
            kvc_ref[key_width + g * HEAD_SIZE : key_width + (g + 1) * HEAD_SIZE, :]
            .astype(jnp.float32)
            .T.astype(jnp.bfloat16)
        )
    bias_ref[...] = range_bias(low_ref, high_ref, kept, rows)
    d_k_ref[...] = jnp.zeros_like(d_k_ref)
    d_v_ref[...] = jnp.zeros_like(d_v_ref)

    def pair(c, carry):
        d_o_pair = d_o_ref[:, pl.ds(pl.multiple_of(c * 2 * HEAD_SIZE, 2 * HEAD_SIZE), 2 * HEAD_SIZE)]
        d_o_wide = d_o_pair.astype(jnp.float32).T
        pair_at = pl.multiple_of(c * 2 * HEAD_SIZE, 2 * HEAD_SIZE)
        q_rows = q_ref[pl.ds(pair_at, 2 * HEAD_SIZE), :].astype(jnp.float32).T.astype(jnp.bfloat16)
        for j in range(2):
            h = 2 * c + j
            g = h // head_groups
            at = pl.multiple_of(h * HEAD_SIZE, HEAD_SIZE)
            part = slice(j * HEAD_SIZE, (j + 1) * HEAD_SIZE)
            d_o_t = d_o_wide[part]
            delta = jnp.sum(d_o_t * attn_ref[pl.ds(at, HEAD_SIZE), :], 0, keepdims=True)
            s = jnp.dot(
                k_ref[g], q_ref[pl.ds(at, HEAD_SIZE), :], preferred_element_type=jnp.float32
            )
            p = jnp.exp(s + bias_ref[...] - lse_ref[h])
            d_p = jnp.dot(
                v_ref[g], d_o_t.astype(jnp.bfloat16), preferred_element_type=jnp.float32
            )
            d_s = (p * (d_p - delta)).astype(jnp.bfloat16)
            d_v_ref[g] += jnp.dot(
                p.astype(jnp.bfloat16), d_o_pair[:, part], preferred_element_type=jnp.float32
            )
            d_k_ref[g] += jnp.dot(d_s, q_rows[:, part], preferred_element_type=jnp.float32)
            k_at = pl.multiple_of(g * HEAD_SIZE, HEAD_SIZE)
            d_q = jnp.dot(
                kvc_ref[pl.ds(k_at, HEAD_SIZE), :], d_s, preferred_element_type=jnp.float32
            )
            d_q_ref[pl.ds(at, HEAD_SIZE), :] = turn(
                d_q * HEAD_SIZE**-0.5, cos_ref[...], -sin_ref[...]
            ).astype(jnp.bfloat16)
        return carry

    lax.fori_loop(0, QUERY_HEADS // 2, pair, 0)
    halves = [d_k_ref[g].T for g in range(KEY_VALUE_HEADS)]
    halves = halves + [d_v_ref[g].T for g in range(KEY_VALUE_HEADS)]
    packed = jnp.concatenate(halves, 0).astype(jnp.bfloat16)
    for e in range(shards):
        d_kv_ref[e] = lax.dot_general(
            packed,
            pick_rows(meta_ref, e, slots, kept),
            (((1,), (1,)), ((), ())),
            preferred_element_type=jnp.float32,
        ).astype(jnp.bfloat16)


def attend_back(meta, low, high, q, kvc, d_o, attn, lse, cosine, sine):
    both, kept = kvc.shape
    width, rows = q.shape
    shards = meta.shape[1]
    whole = pl.BlockSpec(memory_space=pltpu.VMEM)
    per_head = (KEY_VALUE_HEADS, kept, HEAD_SIZE)
    return pl.pallas_call(
        attend_back_kernel,
        out_shape=(
            jax.ShapeDtypeStruct((width, rows), jnp.bfloat16),
            jax.ShapeDtypeStruct((shards, both, rows), jnp.bfloat16),
        ),
        in_specs=[pl.BlockSpec(memory_space=pltpu.SMEM)] + [whole] * 9,
        out_specs=(whole,) * 2,
        scratch_shapes=[
            pltpu.VMEM((kept, rows), jnp.float32),
            pltpu.VMEM(per_head, jnp.bfloat16),
            pltpu.VMEM(per_head, jnp.bfloat16),
            pltpu.VMEM(per_head, jnp.float32),
            pltpu.VMEM(per_head, jnp.float32),
        ],
        compiler_params=pltpu.CompilerParams(vmem_limit_bytes=ATTEND_BYTES),
        cost_estimate=pl.CostEstimate(
            flops=10 * width * rows * kept * 4,
            bytes_accessed=width * rows * 12,
            transcendentals=QUERY_HEADS * rows * kept,
        ),
        name="attend_back",
    )(meta, low, high, q, kvc, d_o, attn, lse, cosine, sine)


def body(
    tokens,
    cotangent,
    counts,
    lengths,
    attn_gain,
    w_query,
    b_query,
    w_key,
    w_value,
    b_value,
    w_out,
    mlp_gain,
    w_gate,
    w_up,
    w_down,
):
    lanes = lax.axis_size("dp")
    fsdp_size = lax.axis_size("fsdp")
    token_rows, width = tokens.shape[1:]
    inputs = tokens[0].astype(jnp.float32)
    valid, position, low, high, meta = own_slots(
        counts[0], lengths[0], lax.axis_index("fsdp"), token_rows
    )
    valid_col = valid.astype(jnp.float32)[:, None]
    query_part, key_part, out_part = w_query.shape[1], w_key.shape[1], w_out.shape[1]
    hidden_part = w_gate.shape[1]
    pieces_each = lanes // fsdp_size
    query_width, key_width = QUERY_HEADS * HEAD_SIZE, KEY_VALUE_HEADS * HEAD_SIZE
    rows_each = w_gate.shape[0]

    projections = (
        gather_rows(jnp.concatenate([w_query, w_key, w_value, w_out], 1), fsdp_size)
        .reshape(width, -1)
        .T
    )
    joint_rows = projections.shape[0]
    vector_row = jnp.concatenate([attn_gain, b_query, b_value, mlp_gain])
    vector_count = vector_row.shape[0]
    vector_block = jnp.zeros((16, width), jnp.bfloat16).at[0, :vector_count].set(vector_row)
    own_block = jnp.concatenate([projections, vector_block])
    blocks = run(gather_steps(own_block, lanes))
    down_t = w_down.T.reshape(out_part, pieces_each, hidden_part).transpose(1, 0, 2)
    hidden_own = jnp.concatenate([w_gate, w_up, down_t.reshape(-1, hidden_part)])
    hidden_slabs = lax.all_gather(hidden_own, "fsdp", axis=0)
    gate_w = hidden_slabs[:, :rows_each].reshape(width, hidden_part)
    up_w = hidden_slabs[:, rows_each : 2 * rows_each].reshape(width, hidden_part)
    down_slabs = hidden_slabs[:, 2 * rows_each :]
    grad_out = cotangent[0].astype(jnp.float32)
    d_down = (valid_col * grad_out).astype(jnp.bfloat16)
    d_down, blocks = lax.optimization_barrier((d_down, blocks))
    d_down_moves = gather_steps(d_down, lanes)
    d_down_near, _ = next(d_down_moves)
    down_moves = exchange_steps(down_slabs.reshape(lanes, out_part, hidden_part), lanes)
    down_near, _ = next(down_moves)

    edges = (0, query_part, query_part + key_part, query_part + 2 * key_part, joint_rows)
    if lanes == 8:
        joint_t, wo_t, vector_table = assemble(blocks, query_part, key_part)
        vector_table = vector_table[:, 0, :vector_count].astype(jnp.float32)
    else:
        spread = jnp.stack(blocks)
        joint_t = jnp.concatenate(
            [spread[:, edges[i] : edges[i + 1]].reshape(-1, width) for i in range(3)]
        )
        wo_t = spread[:, edges[3] : edges[4]].reshape(-1, width)
        vector_table = spread[:, joint_rows, :vector_count].astype(jnp.float32)
    marks = [0]
    for size in (query_part, query_part, key_part, query_part):
        marks.append(marks[-1] + size)
    gain_one, query_bias, value_bias, gain_two = [
        vector_table[:, marks[i] : marks[i + 1]].reshape(-1) for i in range(4)
    ]

    inv_one = lax.rsqrt(jnp.mean(inputs * inputs, -1, keepdims=True) + EPS)
    unit_one = inputs * inv_one
    normed = (unit_one * gain_one).astype(jnp.bfloat16)
    cosine, sine = rope_tables(position.astype(jnp.float32), HEAD_SIZE // 2)
    query_rows, pair_rows = project(normed, joint_t, query_bias, value_bias, cosine, sine)
    d_down_near, pair_rows = tie(d_down_near, pair_rows)
    d_down_far, _ = d_down_moves.send(d_down_near)
    gathered = gather_earlier(pair_rows, fsdp_size)
    d_down_far, gathered = tie(d_down_far, gathered)
    d_down_pieces = finish(d_down_moves, d_down_far)
    heads_out, attention, log_total, packed_kv = attend(
        meta, low[None], high[None], query_rows, gathered
    )
    down_near, heads_out = tie(down_near, heads_out)
    down_w = finish(down_moves, down_near).reshape(width, hidden_part)
    proj = dot_nt(heads_out, wo_t)
    hidden = inputs + valid_col * proj
    inv_two = lax.rsqrt(jnp.mean(hidden * hidden, -1, keepdims=True) + EPS)
    unit_two = hidden * inv_two
    normed2 = (unit_two * gain_two).astype(jnp.bfloat16)

    normed2, down_w = tie(normed2, down_w)
    results = [[], [], [], [], []]

    def feed_more(pieces, cotangents):
        for first in range(0, len(pieces), 2):
            piece = slice(first, first + 2)
            found = feed(pieces[piece], cotangents[piece], gate_w, up_w, down_w)
            for group, values in zip(results, found):
                group.extend(values)

    moves = gather_steps(normed2, lanes)
    near, ready = next(moves)
    feed_more(ready, d_down_pieces[:2])
    near, results = tie(near, results)
    far, ready = moves.send(near)
    feed_more(ready, d_down_pieces[2 : lanes - 2])
    far, results = tie(far, results)
    normed2_pieces = finish(moves, far)
    feed_more(normed2_pieces[lanes - 2 :], d_down_pieces[lanes - 2 :])
    acts, d_gates, d_ups, d_n2_parts, down_parts = results
    grad_down = weight_grad(d_down_pieces, acts, lanes)
    grad_gate = weight_grad(normed2_pieces, d_gates, lanes)
    grad_up = weight_grad(normed2_pieces, d_ups, lanes)
    moves = scatter_steps(d_n2_parts, lanes)
    far, _ = next(moves)
    far, grad_down = tie(far, grad_down)
    near, _ = moves.send(far)
    near, (grad_gate, grad_up) = tie(near, (grad_gate, grad_up))
    d_n2 = finish(moves, near)
    (down_parts, grad_down), d_n2 = tie((down_parts, grad_down), d_n2)
    down_moves = scatter_steps(down_parts, lanes)
    down_far, _ = next(down_moves)
    grad_moves = exchange_steps(grad_down.reshape(lanes, out_part, hidden_part), lanes)
    grad_near, _ = next(grad_moves)
    pair_grads = jnp.concatenate(
        [
            grad_gate.reshape(fsdp_size, rows_each, hidden_part),
            grad_up.reshape(fsdp_size, rows_each, hidden_part),
        ],
        1,
    )

    scaled_two = d_n2 * gain_two
    dh = grad_out + inv_two * (
        scaled_two - unit_two * jnp.mean(scaled_two * unit_two, -1, keepdims=True)
    )
    grad_gain_two = jnp.sum(d_n2 * unit_two, 0)
    d_proj = (valid_col * dh).astype(jnp.bfloat16)
    pair_sums = lax.psum_scatter(
        pair_grads, "fsdp", scatter_dimension=0, tiled=False
    ).astype(jnp.float32)
    grad_w_gate = pair_sums[:rows_each]
    grad_w_up = pair_sums[rows_each:]
    out_grad = lax.psum_scatter(
        dot_tn(d_proj, heads_out).astype(jnp.bfloat16).reshape(lanes, out_part, -1),
        "dp",
        scatter_dimension=0,
        tiled=False,
    )
    head_gradient = dot_nn(d_proj, wo_t).astype(jnp.bfloat16)
    d_q_pre, d_kv = attend_back(
        meta,
        low[None],
        high[None],
        query_rows,
        packed_kv,
        head_gradient,
        attention,
        log_total,
        cosine,
        sine,
    )
    (grad_near, down_far), d_kv = tie((grad_near, down_far), d_kv)
    grad_down = finish(grad_moves, grad_near)
    down_near, _ = down_moves.send(down_far)
    own_kv = scatter_earlier(d_kv, fsdp_size)
    down_near, own_kv = tie(down_near, own_kv)
    down = finish(down_moves, down_near)
    mixed = (hidden + valid_col * down).astype(jnp.bfloat16)
    grad_w_down = (
        lax.psum_scatter(
            grad_down.reshape(fsdp_size, rows_each, hidden_part),
            "fsdp",
            scatter_dimension=0,
            tiled=False,
        )
        .astype(jnp.float32)
        .reshape(pieces_each, out_part, hidden_part)
        .transpose(0, 2, 1)
        .reshape(-1, out_part)
    )
    d_k_pre = rotary_reverse(own_kv[:key_width], cosine, sine).astype(jnp.bfloat16)
    d_v_pre = own_kv[key_width:].astype(jnp.bfloat16)
    d_joint = jnp.concatenate([d_q_pre, d_k_pre, d_v_pre])
    d_n1 = dot_tn(d_joint, joint_t)
    scaled_one = d_n1 * gain_one
    d_tokens = (
        dh + inv_one * (scaled_one - unit_one * jnp.mean(scaled_one * unit_one, -1, keepdims=True))
    ).astype(jnp.bfloat16)
    local_vectors = (
        jnp.sum(d_n1 * unit_one, 0),
        jnp.sum(d_q_pre.astype(jnp.float32), 1),
        jnp.sum(d_v_pre.astype(jnp.float32), 1),
        grad_gain_two,
    )
    vector_rows = jnp.concatenate([v.reshape(lanes, -1) for v in local_vectors], 1)
    vector_rows = jnp.pad(vector_rows, ((0, 0), (0, width - vector_count)))
    vector_rows = jnp.pad(vector_rows[:, None].astype(jnp.bfloat16), ((0, 0), (0, 15), (0, 0)))
    joint_grads = dot_nn(d_joint, normed).astype(jnp.bfloat16)
    joint_parts = jnp.concatenate(
        [
            joint_grads[:query_width].reshape(lanes, query_part, width),
            joint_grads[query_width : query_width + key_width].reshape(lanes, key_part, width),
            joint_grads[query_width + key_width :].reshape(lanes, key_part, width),
            vector_rows,
        ],
        1,
    )
    joint_sum = run(scatter_steps([joint_parts[e] for e in range(lanes)], lanes, ordered=True))
    qkv_rows = query_part + 2 * key_part
    row_sums = scatter_rows(
        jnp.concatenate([joint_sum[:qkv_rows].astype(jnp.bfloat16), out_grad])
        .T.reshape(fsdp_size, rows_each, joint_rows),
        fsdp_size,
    )
    grad_w_query, grad_w_key, grad_w_value, out_grad = [
        row_sums[:, edges[i] : edges[i + 1]] for i in range(4)
    ]
    own_vectors = joint_sum[qkv_rows, :vector_count]
    vector_sum = own_vectors
    for k in range(1, fsdp_size):
        vector_sum = vector_sum + lax.ppermute(
            own_vectors, "fsdp", [(i, (i + k) % fsdp_size) for i in range(fsdp_size)]
        )
    vector_pieces = [vector_sum[marks[i] : marks[i + 1]] for i in range(4)]
    return (
        mixed[None],
        d_tokens[None],
        vector_pieces[0],
        grad_w_query,
        vector_pieces[1],
        grad_w_key,
        grad_w_value,
        vector_pieces[2],
        out_grad,
        vector_pieces[3],
        grad_w_gate,
        grad_w_up,
        grad_w_down,
    )


def solution(mesh):
    placed = (
        P("dp", "fsdp", None),
        P("dp", "fsdp", None),
        P("dp", None),
        P("dp", None),
        P("dp"),
        P("fsdp", "dp"),
        P("dp"),
        P("fsdp", "dp"),
        P("fsdp", "dp"),
        P("dp"),
        P("fsdp", "dp"),
        P("dp"),
        P("fsdp", "dp"),
        P("fsdp", "dp"),
        P("fsdp", "dp"),
    )
    return jax.shard_map(
        body,
        mesh=mesh,
        in_specs=placed,
        out_specs=(
            P("dp", "fsdp", None),
            P("dp", "fsdp", None),
            P("dp"),
            P("fsdp", "dp"),
            P("dp"),
            P("fsdp", "dp"),
            P("fsdp", "dp"),
            P("dp"),
            P("fsdp", "dp"),
            P("dp"),
            P("fsdp", "dp"),
            P("fsdp", "dp"),
            P("fsdp", "dp"),
        ),
        check_vma=False,
    )
```

```python
import functools

import jax
import jax.numpy as jnp
from jax import lax
from jax.experimental import pallas as pl
from jax.experimental.pallas import tpu as pltpu
from jax.sharding import PartitionSpec as P

QUERY_HEADS = 14
KEY_VALUE_HEADS = 2
HEAD_SIZE = 64
KERNEL_BYTES = 12 * 2**20


EPS = 1e-06
THETA = 1000000.0
NEGATIVE_FILL = -1e30


def own_slots(count_row, length_row, place, slots):
    before = jnp.cumsum(count_row) - count_row
    inner = jnp.arange(slots, dtype=jnp.int32)
    valid = inner < count_row[place]
    index = before[place] + inner
    ends = jnp.cumsum(length_row)
    numbers = jnp.sum((index[:, None] >= ends[None, :]).astype(jnp.int32), 1)
    starts = ends - length_row
    owners = jnp.arange(length_row.shape[0], dtype=jnp.int32)
    start_of = jnp.sum(
        (numbers[:, None] == owners[None, :]).astype(jnp.int32) * starts[None, :], 1
    )
    position = jnp.where(valid, index - start_of, 0)
    opened = jnp.max(jnp.where(index[:, None] >= ends[None, :], ends[None, :], 0), 1)
    low = jnp.where(valid, opened, 0)
    high = jnp.where(valid, index, 0)
    return valid, position, low, high, jnp.stack([count_row, before])


def rope_tables(position, half):
    steps = jnp.arange(half, dtype=jnp.float32) * (1.0 / half)
    freq = THETA ** (-steps)
    angle = freq[:, None] * position[None, :]
    return jnp.cos(angle), jnp.sin(angle)


def rotary_apply(rows, cosine, sine):
    cube = rows.reshape(-1, 2, HEAD_SIZE // 2, rows.shape[1])
    first, second = cube[:, 0], cube[:, 1]
    turned = [first * cosine - second * sine, second * cosine + first * sine]
    return jnp.stack(turned, 1).reshape(rows.shape)


def rotary_reverse(rows, cosine, sine):
    return rotary_apply(rows, cosine, -sine)


def flip(array, mask, size):
    return lax.ppermute(array, "dp", [(i, i ^ mask) for i in range(size)])


def tie(first, second):
    return lax.optimization_barrier((first, second))


def finish(steps, pending):
    try:
        steps.send(pending)
    except StopIteration as end:
        return end.value


def run(steps):
    try:
        pending = next(steps)
        while True:
            pending = steps.send(pending[0])
    except StopIteration as end:
        return end.value


def gather_steps(rows, size):
    if size != 8:
        whole = lax.all_gather(rows, "dp", axis=0)
        pieces = [whole[k] for k in range(size)]
        yield (), pieces[:2]
        yield (), pieces[2 : size - 2]
        return pieces
    half = rows.shape[0] // 2
    by_x, by_y, by_core = flip(rows, 2, 8), flip(rows, 4, 8), flip(rows, 1, 8)
    by_x, by_y = yield (by_x, by_y), [rows, by_core]
    far_a, far_b = flip(by_x[:half], 4, 8), flip(by_y[half:], 2, 8)
    core_x, core_y = flip(by_x, 1, 8), flip(by_y, 1, 8)
    far_a, far_b = yield (far_a, far_b), [by_x, core_x, by_y, core_y]
    far = jnp.concatenate([far_a, far_b])
    return [rows, by_core, by_x, core_x, by_y, core_y, far, flip(far, 1, 8)]


def scatter_steps(parts, size, ordered=False):
    if size != 8:
        total = lax.psum_scatter(jnp.stack(parts), "dp", scatter_dimension=0, tiled=False)
        yield (), None
        yield (), None
        return total.astype(jnp.float32)
    if ordered:
        place = lax.axis_index("dp")
        parts = jnp.stack(parts)
        parts = [lax.dynamic_index_in_dim(parts, place ^ k, 0, False) for k in range(8)]
    half = parts[0].shape[0] // 2
    wide = jnp.float32
    seven, five, three, one = [flip(parts[k], 1, 8) for k in (7, 5, 3, 1)]
    far = (parts[6].astype(wide) + seven.astype(wide)).astype(jnp.bfloat16)
    far_x, far_y = yield (flip(far[:half], 2, 8), flip(far[half:], 4, 8)), None
    on_y = parts[4].astype(wide) + five.astype(wide)
    on_x = parts[2].astype(wide) + three.astype(wide)
    on_y = jnp.concatenate([on_y[:half] + far_x.astype(wide), on_y[half:]]).astype(jnp.bfloat16)
    on_x = jnp.concatenate([on_x[:half], on_x[half:] + far_y.astype(wide)]).astype(jnp.bfloat16)
    got_x, got_y = yield (flip(on_x, 2, 8), flip(on_y, 4, 8)), None
    own = parts[0].astype(wide) + one.astype(wide)
    return own + got_x.astype(wide) + got_y.astype(wide)


def exchange_steps(parts, size):
    if size != 8:
        result = lax.all_to_all(parts, "dp", 0, 0, tiled=True)
        yield (), None
        return result
    place = lax.axis_index("dp")
    chip, core = place // 2, place % 2
    block = parts.reshape((4, 2) + parts.shape[1:])
    kept = lax.dynamic_index_in_dim(block, core, 1, True)
    got = flip(lax.dynamic_index_in_dim(block, 1 - core, 1, True), 1, 8)
    block = jnp.where(
        core == 0, jnp.concatenate([kept, got], 1), jnp.concatenate([got, kept], 1)
    )
    moved = tuple(
        flip(lax.dynamic_index_in_dim(block, chip ^ k, 0, True), 2 * k, 8) for k in (1, 2, 3)
    )
    moved = yield moved, None
    for k in (1, 2, 3):
        block = lax.dynamic_update_slice_in_dim(block, moved[k - 1], chip ^ k, 0)
    return block.reshape(parts.shape)


def gather_rows(rows, size):
    place = lax.axis_index("fsdp")
    result = jnp.zeros((size,) + rows.shape, rows.dtype)
    result = lax.dynamic_update_slice_in_dim(result, rows[None], place, 0)
    for k in range(1, size):
        piece = lax.ppermute(rows, "fsdp", [(i, (i + k) % size) for i in range(size)])
        result = lax.dynamic_update_slice_in_dim(result, piece[None], (place + size - k) % size, 0)
    return result


def scatter_rows(parts, size):
    place = lax.axis_index("fsdp")
    sent = parts.astype(jnp.bfloat16)
    total = lax.dynamic_index_in_dim(parts, place, 0, False).astype(jnp.float32)
    for k in range(1, size):
        piece = lax.dynamic_index_in_dim(sent, (place + k) % size, 0, False)
        total = total + lax.ppermute(
            piece, "fsdp", [(i, (i + k) % size) for i in range(size)]
        ).astype(jnp.float32)
    return total


def gather_earlier(rows, size):
    place = lax.axis_index("fsdp")
    result = jnp.zeros((size,) + rows.shape, rows.dtype)
    result = lax.dynamic_update_slice_in_dim(result, rows[None], place, 0)
    for k in range(1, size):
        piece = lax.ppermute(rows, "fsdp", [(i, i + k) for i in range(size - k)])
        result = lax.dynamic_update_slice_in_dim(result, piece[None], (place + size - k) % size, 0)
    return result


def scatter_earlier(parts, size):
    place = lax.axis_index("fsdp")
    total = lax.dynamic_index_in_dim(parts, place, 0, False).astype(jnp.float32)
    for k in range(1, size):
        piece = lax.dynamic_index_in_dim(parts, (place + size - k) % size, 0, False)
        total = total + lax.ppermute(
            piece, "fsdp", [(i, i - k) for i in range(k, size)]
        ).astype(jnp.float32)
    return total


def dot_tn(left, right):
    return lax.dot_general(
        left, right, (((0,), (0,)), ((), ())), preferred_element_type=jnp.float32
    )


def dot_nt(left, right):
    return lax.dot_general(
        left, right, (((1,), (1,)), ((), ())), preferred_element_type=jnp.float32
    )


def dot_nn(left, right):
    return jnp.dot(left, right, preferred_element_type=jnp.float32)


def assemble_kernel(place_ref, *refs):
    pieces, (joint_ref, out_ref, vector_ref) = refs[:8], refs[8:]
    width = out_ref.shape[1]
    query_part = out_ref.shape[0] // 8
    key_part = (joint_ref.shape[0] - out_ref.shape[0]) // 16
    lead = 2 * key_part + query_part
    key_from, value_from = 8 * query_part, 8 * (query_part + key_part)
    for k in range(8):
        e = jnp.bitwise_xor(place_ref[0], k)
        piece = pieces[k]
        joint_ref[pl.ds(pl.multiple_of(e * query_part, 16), query_part), :] = piece[:query_part]
        joint_ref[pl.ds(pl.multiple_of(key_from + e * key_part, 16), key_part), :] = piece[
            query_part : query_part + key_part
        ]
        joint_ref[pl.ds(pl.multiple_of(value_from + e * key_part, 16), key_part), :] = piece[
            query_part + key_part : lead
        ]
        out_ref[pl.ds(pl.multiple_of(e * query_part, 16), query_part), :] = piece[
            lead : lead + query_part
        ]
        vector_ref[e] = piece[lead + query_part :]


def assemble(pieces, query_part, key_part):
    width = pieces[0].shape[1]
    vector_rows = pieces[0].shape[0] - 2 * query_part - 2 * key_part
    whole = pl.BlockSpec(memory_space=pltpu.VMEM)
    return pl.pallas_call(
        assemble_kernel,
        out_shape=(
            jax.ShapeDtypeStruct((8 * (query_part + 2 * key_part), width), jnp.bfloat16),
            jax.ShapeDtypeStruct((8 * query_part, width), jnp.bfloat16),
            jax.ShapeDtypeStruct((8, vector_rows, width), jnp.bfloat16),
        ),
        in_specs=[pl.BlockSpec(memory_space=pltpu.SMEM)] + [whole] * 8,
        out_specs=(whole,) * 3,
        compiler_params=pltpu.CompilerParams(vmem_limit_bytes=KERNEL_BYTES),
        name="assemble",
    )(lax.axis_index("dp").reshape(1), *pieces)


def turn(rows, cosine, sine):
    half = HEAD_SIZE // 2
    first, second = rows[:half], rows[half:]
    return jnp.concatenate([first * cosine - second * sine, second * cosine + first * sine])


def project_kernel(x_ref, w_ref, q_bias_ref, v_bias_ref, cos_ref, sin_ref, q_ref, kv_ref):
    cosine, sine = cos_ref[...], sin_ref[...]
    joint = lax.dot_general(
        w_ref[...], x_ref[...], (((1,), (1,)), ((), ())), preferred_element_type=jnp.float32
    )
    for h in range(QUERY_HEADS):
        at = slice(h * HEAD_SIZE, (h + 1) * HEAD_SIZE)
        rows = turn(joint[at] + q_bias_ref[at], cosine, sine).astype(jnp.bfloat16)
        q_ref[at] = rows * jnp.bfloat16(HEAD_SIZE**-0.5)
    for g in range(KEY_VALUE_HEADS):
        at = slice(g * HEAD_SIZE, (g + 1) * HEAD_SIZE)
        first = (QUERY_HEADS + g) * HEAD_SIZE
        kv_ref[at] = turn(joint[first : first + HEAD_SIZE], cosine, sine).astype(jnp.bfloat16)
    key_width = KEY_VALUE_HEADS * HEAD_SIZE
    kv_ref[key_width:] = (
        joint[QUERY_HEADS * HEAD_SIZE + key_width :] + v_bias_ref[...]
    ).astype(jnp.bfloat16)


def project(normed, joint_t, query_bias, value_bias, cosine, sine):
    rows = normed.shape[0]
    whole = pl.BlockSpec(memory_space=pltpu.VMEM)
    query_width, key_width = QUERY_HEADS * HEAD_SIZE, KEY_VALUE_HEADS * HEAD_SIZE
    return pl.pallas_call(
        project_kernel,
        out_shape=(
            jax.ShapeDtypeStruct((query_width, rows), jnp.bfloat16),
            jax.ShapeDtypeStruct((2 * key_width, rows), jnp.bfloat16),
        ),
        in_specs=[whole] * 6,
        out_specs=(whole,) * 2,
        compiler_params=pltpu.CompilerParams(vmem_limit_bytes=KERNEL_BYTES),
        name="project",
    )(normed, joint_t, query_bias[:, None], value_bias[:, None], cosine, sine)


def feed_kernel(count, *refs):
    xs, ds = refs[:count], refs[count : 2 * count]
    gate_ref, up_ref, down_ref = refs[2 * count : 2 * count + 3]
    outs = refs[2 * count + 3 :]
    acts, d_gates, d_ups, d_xs, downs = [outs[i * count : (i + 1) * count] for i in range(5)]
    across = (((1,), (1,)), ((), ()))
    for k in range(count):
        x = xs[k][...]
        gate = jnp.dot(x, gate_ref[...], preferred_element_type=jnp.float32)
        up = jnp.dot(x, up_ref[...], preferred_element_type=jnp.float32)
        d_act = jnp.dot(ds[k][...], down_ref[...], preferred_element_type=jnp.float32)
        sigma = jax.nn.sigmoid(gate)
        silu = gate * sigma
        act = (silu * up).astype(jnp.bfloat16)
        d_gate = (d_act * up * sigma * (1.0 + gate * (1.0 - sigma))).astype(jnp.bfloat16)
        d_up = (d_act * silu).astype(jnp.bfloat16)
        acts[k][...] = act
        d_gates[k][...] = d_gate
        d_ups[k][...] = d_up
        d_x = lax.dot_general(d_gate, gate_ref[...], across, preferred_element_type=jnp.float32)
        d_x = d_x + lax.dot_general(
            d_up, up_ref[...], across, preferred_element_type=jnp.float32
        )
        d_xs[k][...] = d_x.astype(jnp.bfloat16)
        downs[k][...] = lax.dot_general(
            act, down_ref[...], across, preferred_element_type=jnp.float32
        ).astype(jnp.bfloat16)


def feed(xs, ds, gate_w, up_w, down_w):
    count = len(xs)
    rows, width = xs[0].shape
    hidden = gate_w.shape[1]
    whole = pl.BlockSpec(memory_space=pltpu.VMEM)
    narrow = jax.ShapeDtypeStruct((rows, hidden), jnp.bfloat16)
    wide = jax.ShapeDtypeStruct((rows, width), jnp.bfloat16)
    outs = pl.pallas_call(
        functools.partial(feed_kernel, count),
        out_shape=(narrow,) * (3 * count) + (wide,) * (2 * count),
        in_specs=[whole] * (2 * count + 3),
        out_specs=(whole,) * (5 * count),
        compiler_params=pltpu.CompilerParams(vmem_limit_bytes=KERNEL_BYTES),
        cost_estimate=pl.CostEstimate(
            flops=14 * count * rows * width * hidden,
            bytes_accessed=count * rows * (8 * width + 6 * hidden),
            transcendentals=count * rows * hidden,
        ),
        name="feed",
    )(*xs, *ds, gate_w, up_w, down_w)
    return [outs[i * count : (i + 1) * count] for i in range(5)]


def grad_kernel(count, *refs):
    lefts, rights, out_ref, total_ref = refs[:count], refs[count : 2 * count], refs[-2], refs[-1]
    for k in range(count):
        term = lax.dot_general(
            lefts[k][...],
            rights[k][...],
            (((0,), (0,)), ((), ())),
            preferred_element_type=jnp.float32,
        )
        if k == 0:
            total_ref[...] = term
        elif k < count - 1:
            total_ref[...] += term
        else:
            out_ref[...] = (total_ref[...] + term).astype(jnp.bfloat16)


def weight_grad(lefts, rights, size):
    if size != 8:
        return dot_tn(jnp.concatenate(lefts), jnp.concatenate(rights)).astype(jnp.bfloat16)
    rows, width = lefts[0].shape
    hidden = rights[0].shape[1]
    whole = pl.BlockSpec(memory_space=pltpu.VMEM)
    return pl.pallas_call(
        functools.partial(grad_kernel, size),
        out_shape=jax.ShapeDtypeStruct((width, hidden), jnp.bfloat16),
        in_specs=[whole] * (2 * size),
        out_specs=whole,
        scratch_shapes=[pltpu.VMEM((width, hidden), jnp.float32)],
        compiler_params=pltpu.CompilerParams(vmem_limit_bytes=KERNEL_BYTES),
        cost_estimate=pl.CostEstimate(
            flops=2 * size * rows * width * hidden,
            bytes_accessed=2 * size * rows * (width + hidden),
            transcendentals=0,
        ),
        name="weight_grad",
    )(*lefts, *rights)


def pick_rows(meta_ref, e, slots, kept):
    slot = lax.broadcasted_iota(jnp.int32, (slots, kept), 0)
    index = lax.broadcasted_iota(jnp.int32, (slots, kept), 1)
    chosen = (slot + meta_ref[1, e] == index) & (slot < meta_ref[0, e])
    return jnp.where(chosen, 1.0, 0.0).astype(jnp.bfloat16)


def range_bias(low_ref, high_ref, kept, rows):
    index = lax.broadcasted_iota(jnp.int32, (kept, rows), 0)
    inside = (index >= low_ref[...]) & (index <= high_ref[...])
    return jnp.where(inside, 0.0, NEGATIVE_FILL)


def attend_kernel(
    meta_ref, low_ref, high_ref, q_ref, kv_ref, o_ref, attn_ref, lse_ref, kvc_ref, bias_ref, k_ref
):
    shards, both, slots = kv_ref.shape
    kept, rows = bias_ref.shape
    head_groups = QUERY_HEADS // KEY_VALUE_HEADS
    key_width = both // 2
    packed = jnp.zeros((both, kept), jnp.float32)
    for e in range(shards):
        packed = packed + jnp.dot(
            kv_ref[e], pick_rows(meta_ref, e, slots, kept), preferred_element_type=jnp.float32
        )
    kvc_ref[...] = packed.astype(jnp.bfloat16)
    for g in range(KEY_VALUE_HEADS):
        k_ref[g] = packed[g * HEAD_SIZE : (g + 1) * HEAD_SIZE].T.astype(jnp.bfloat16)
    bias_ref[...] = range_bias(low_ref, high_ref, kept, rows)

    def pair(c, carry):
        found = []
        for j in range(2):
            h = 2 * c + j
            g = h // head_groups
            at = pl.multiple_of(h * HEAD_SIZE, HEAD_SIZE)
            s = jnp.dot(
                k_ref[g], q_ref[pl.ds(at, HEAD_SIZE), :], preferred_element_type=jnp.float32
            )
            s = s + bias_ref[...]
            top = jnp.max(s, 0, keepdims=True)
            p = jnp.exp(s - top)
            total = jnp.sum(p, 0, keepdims=True)
            v_at = pl.multiple_of(key_width + g * HEAD_SIZE, HEAD_SIZE)
            out = jnp.dot(
                kvc_ref[pl.ds(v_at, HEAD_SIZE), :],
                p.astype(jnp.bfloat16),
                preferred_element_type=jnp.float32,
            )
            out = out / total
            attn_ref[pl.ds(at, HEAD_SIZE), :] = out
            lse_ref[h] = top + jnp.log(total)
            found.append(out)
        block = jnp.concatenate(found, 0).T
        o_ref[:, pl.ds(pl.multiple_of(c * 2 * HEAD_SIZE, 2 * HEAD_SIZE), 2 * HEAD_SIZE)] = (
            block.astype(jnp.bfloat16)
        )
        return carry

    lax.fori_loop(0, QUERY_HEADS // 2, pair, 0)


def attend(meta, low, high, q, kv):
    shards, both, slots = kv.shape
    kept = shards * slots * 3 // 4
    width, rows = q.shape
    whole = pl.BlockSpec(memory_space=pltpu.VMEM)
    return pl.pallas_call(
        attend_kernel,
        out_shape=(
            jax.ShapeDtypeStruct((rows, width), jnp.bfloat16),
            jax.ShapeDtypeStruct((width, rows), jnp.float32),
            jax.ShapeDtypeStruct((QUERY_HEADS, 1, rows), jnp.float32),
            jax.ShapeDtypeStruct((both, kept), jnp.bfloat16),
        ),
        in_specs=[pl.BlockSpec(memory_space=pltpu.SMEM)] + [whole] * 4,
        out_specs=(whole,) * 4,
        scratch_shapes=[
            pltpu.VMEM((kept, rows), jnp.float32),
            pltpu.VMEM((KEY_VALUE_HEADS, kept, HEAD_SIZE), jnp.bfloat16),
        ],
        compiler_params=pltpu.CompilerParams(vmem_limit_bytes=KERNEL_BYTES + 32 * kept * rows),
        cost_estimate=pl.CostEstimate(
            flops=4 * width * rows * kept * 4,
            bytes_accessed=width * rows * 8,
            transcendentals=QUERY_HEADS * rows * kept,
        ),
        name="attend",
    )(meta, low, high, q, kv)


def attend_back_kernel(
    meta_ref,
    low_ref,
    high_ref,
    q_ref,
    kvc_ref,
    d_o_ref,
    attn_ref,
    lse_ref,
    cos_ref,
    sin_ref,
    d_q_ref,
    d_kv_ref,
    bias_ref,
    k_ref,
    v_ref,
    d_k_ref,
    d_v_ref,
):
    shards, both, slots = d_kv_ref.shape
    kept, rows = bias_ref.shape
    head_groups = QUERY_HEADS // KEY_VALUE_HEADS
    key_width = both // 2
    for g in range(KEY_VALUE_HEADS):
        k_ref[g] = kvc_ref[g * HEAD_SIZE : (g + 1) * HEAD_SIZE, :].astype(jnp.float32).T.astype(jnp.bfloat16)
        v_ref[g] = (
            kvc_ref[key_width + g * HEAD_SIZE : key_width + (g + 1) * HEAD_SIZE, :]
            .astype(jnp.float32)
            .T.astype(jnp.bfloat16)
        )
    bias_ref[...] = range_bias(low_ref, high_ref, kept, rows)
    d_k_ref[...] = jnp.zeros_like(d_k_ref)
    d_v_ref[...] = jnp.zeros_like(d_v_ref)

    def pair(c, carry):
        d_o_pair = d_o_ref[:, pl.ds(pl.multiple_of(c * 2 * HEAD_SIZE, 2 * HEAD_SIZE), 2 * HEAD_SIZE)]
        d_o_wide = d_o_pair.astype(jnp.float32).T
        pair_at = pl.multiple_of(c * 2 * HEAD_SIZE, 2 * HEAD_SIZE)
        q_rows = q_ref[pl.ds(pair_at, 2 * HEAD_SIZE), :].astype(jnp.float32).T.astype(jnp.bfloat16)
        for j in range(2):
            h = 2 * c + j
            g = h // head_groups
            at = pl.multiple_of(h * HEAD_SIZE, HEAD_SIZE)
            part = slice(j * HEAD_SIZE, (j + 1) * HEAD_SIZE)
            d_o_t = d_o_wide[part]
            delta = jnp.sum(d_o_t * attn_ref[pl.ds(at, HEAD_SIZE), :], 0, keepdims=True)
            s = jnp.dot(
                k_ref[g], q_ref[pl.ds(at, HEAD_SIZE), :], preferred_element_type=jnp.float32
            )
            p = jnp.exp(s + bias_ref[...] - lse_ref[h])
            d_p = jnp.dot(
                v_ref[g], d_o_t.astype(jnp.bfloat16), preferred_element_type=jnp.float32
            )
            d_s = (p * (d_p - delta)).astype(jnp.bfloat16)
            d_v_ref[g] += jnp.dot(
                p.astype(jnp.bfloat16), d_o_pair[:, part], preferred_element_type=jnp.float32
            )
            d_k_ref[g] += jnp.dot(d_s, q_rows[:, part], preferred_element_type=jnp.float32)
            k_at = pl.multiple_of(g * HEAD_SIZE, HEAD_SIZE)
            d_q = jnp.dot(
                kvc_ref[pl.ds(k_at, HEAD_SIZE), :], d_s, preferred_element_type=jnp.float32
            )
            d_q_ref[pl.ds(at, HEAD_SIZE), :] = turn(
                d_q * HEAD_SIZE**-0.5, cos_ref[...], -sin_ref[...]
            ).astype(jnp.bfloat16)
        return carry

    lax.fori_loop(0, QUERY_HEADS // 2, pair, 0)
    halves = [d_k_ref[g].T for g in range(KEY_VALUE_HEADS)]
    halves = halves + [d_v_ref[g].T for g in range(KEY_VALUE_HEADS)]
    packed = jnp.concatenate(halves, 0).astype(jnp.bfloat16)
    for e in range(shards):
        d_kv_ref[e] = lax.dot_general(
            packed,
            pick_rows(meta_ref, e, slots, kept),
            (((1,), (1,)), ((), ())),
            preferred_element_type=jnp.float32,
        ).astype(jnp.bfloat16)


def attend_back(meta, low, high, q, kvc, d_o, attn, lse, cosine, sine):
    both, kept = kvc.shape
    width, rows = q.shape
    shards = meta.shape[1]
    whole = pl.BlockSpec(memory_space=pltpu.VMEM)
    per_head = (KEY_VALUE_HEADS, kept, HEAD_SIZE)
    return pl.pallas_call(
        attend_back_kernel,
        out_shape=(
            jax.ShapeDtypeStruct((width, rows), jnp.bfloat16),
            jax.ShapeDtypeStruct((shards, both, rows), jnp.bfloat16),
        ),
        in_specs=[pl.BlockSpec(memory_space=pltpu.SMEM)] + [whole] * 9,
        out_specs=(whole,) * 2,
        scratch_shapes=[
            pltpu.VMEM((kept, rows), jnp.float32),
            pltpu.VMEM(per_head, jnp.bfloat16),
            pltpu.VMEM(per_head, jnp.bfloat16),
            pltpu.VMEM(per_head, jnp.float32),
            pltpu.VMEM(per_head, jnp.float32),
        ],
        compiler_params=pltpu.CompilerParams(vmem_limit_bytes=KERNEL_BYTES + 32 * kept * rows),
        cost_estimate=pl.CostEstimate(
            flops=10 * width * rows * kept * 4,
            bytes_accessed=width * rows * 12,
            transcendentals=QUERY_HEADS * rows * kept,
        ),
        name="attend_back",
    )(meta, low, high, q, kvc, d_o, attn, lse, cosine, sine)


def body(
    tokens,
    cotangent,
    counts,
    lengths,
    attn_gain,
    w_query,
    b_query,
    w_key,
    w_value,
    b_value,
    w_out,
    mlp_gain,
    w_gate,
    w_up,
    w_down,
):
    lanes = lax.axis_size("dp")
    fsdp_size = lax.axis_size("fsdp")
    token_rows, width = tokens.shape[1:]
    inputs = tokens[0].astype(jnp.float32)
    valid, position, low, high, meta = own_slots(
        counts[0], lengths[0], lax.axis_index("fsdp"), token_rows
    )
    valid_col = valid.astype(jnp.float32)[:, None]
    query_part, key_part, out_part = w_query.shape[1], w_key.shape[1], w_out.shape[1]
    hidden_part = w_gate.shape[1]
    pieces_each = lanes // fsdp_size
    query_width, key_width = QUERY_HEADS * HEAD_SIZE, KEY_VALUE_HEADS * HEAD_SIZE
    rows_each = w_gate.shape[0]

    projections = (
        gather_rows(jnp.concatenate([w_query, w_key, w_value, w_out], 1), fsdp_size)
        .reshape(width, -1)
        .T
    )
    joint_rows = projections.shape[0]
    vector_row = jnp.concatenate([attn_gain, b_query, b_value, mlp_gain])
    vector_count = vector_row.shape[0]
    vector_block = jnp.zeros((16, width), jnp.bfloat16).at[0, :vector_count].set(vector_row)
    own_block = jnp.concatenate([projections, vector_block])
    blocks = run(gather_steps(own_block, lanes))
    down_t = w_down.T.reshape(out_part, pieces_each, hidden_part).transpose(1, 0, 2)
    hidden_own = jnp.concatenate([w_gate, w_up, down_t.reshape(-1, hidden_part)])
    hidden_slabs = lax.all_gather(hidden_own, "fsdp", axis=0)
    gate_w = hidden_slabs[:, :rows_each].reshape(width, hidden_part)
    up_w = hidden_slabs[:, rows_each : 2 * rows_each].reshape(width, hidden_part)
    down_slabs = hidden_slabs[:, 2 * rows_each :]
    grad_out = cotangent[0].astype(jnp.float32)
    d_down = (valid_col * grad_out).astype(jnp.bfloat16)
    d_down, blocks = lax.optimization_barrier((d_down, blocks))
    d_down_moves = gather_steps(d_down, lanes)
    d_down_near, _ = next(d_down_moves)
    down_moves = exchange_steps(down_slabs.reshape(lanes, out_part, hidden_part), lanes)
    down_near, _ = next(down_moves)

    edges = (0, query_part, query_part + key_part, query_part + 2 * key_part, joint_rows)
    if lanes == 8:
        joint_t, wo_t, vector_table = assemble(blocks, query_part, key_part)
        vector_table = vector_table[:, 0, :vector_count].astype(jnp.float32)
    else:
        spread = jnp.stack(blocks)
        joint_t = jnp.concatenate(
            [spread[:, edges[i] : edges[i + 1]].reshape(-1, width) for i in range(3)]
        )
        wo_t = spread[:, edges[3] : edges[4]].reshape(-1, width)
        vector_table = spread[:, joint_rows, :vector_count].astype(jnp.float32)
    marks = [0]
    for size in (query_part, query_part, key_part, query_part):
        marks.append(marks[-1] + size)
    gain_one, query_bias, value_bias, gain_two = [
        vector_table[:, marks[i] : marks[i + 1]].reshape(-1) for i in range(4)
    ]

    inv_one = lax.rsqrt(jnp.mean(inputs * inputs, -1, keepdims=True) + EPS)
    unit_one = inputs * inv_one
    normed = (unit_one * gain_one).astype(jnp.bfloat16)
    cosine, sine = rope_tables(position.astype(jnp.float32), HEAD_SIZE // 2)
    query_rows, pair_rows = project(normed, joint_t, query_bias, value_bias, cosine, sine)
    gathered = gather_earlier(pair_rows, fsdp_size)
    d_down_near, gathered = tie(d_down_near, gathered)
    d_down_far, _ = d_down_moves.send(d_down_near)
    heads_out, attention, log_total, packed_kv = attend(
        meta, low[None], high[None], query_rows, gathered
    )
    (down_near, d_down_far), heads_out = tie((down_near, d_down_far), heads_out)
    d_down_pieces = finish(d_down_moves, d_down_far)
    down_w = finish(down_moves, down_near).reshape(width, hidden_part)
    proj = dot_nt(heads_out, wo_t)
    hidden = inputs + valid_col * proj
    inv_two = lax.rsqrt(jnp.mean(hidden * hidden, -1, keepdims=True) + EPS)
    unit_two = hidden * inv_two
    normed2 = (unit_two * gain_two).astype(jnp.bfloat16)

    normed2, down_w = tie(normed2, down_w)
    results = [[], [], [], [], []]

    def feed_more(pieces, cotangents):
        for first in range(0, len(pieces), 2):
            piece = slice(first, first + 2)
            found = feed(pieces[piece], cotangents[piece], gate_w, up_w, down_w)
            for group, values in zip(results, found):
                group.extend(values)

    moves = gather_steps(normed2, lanes)
    near, ready = next(moves)
    feed_more(ready, d_down_pieces[:2])
    near, results = tie(near, results)
    far, ready = moves.send(near)
    feed_more(ready, d_down_pieces[2 : lanes - 2])
    far, results = tie(far, results)
    normed2_pieces = finish(moves, far)
    feed_more(normed2_pieces[lanes - 2 :], d_down_pieces[lanes - 2 :])
    acts, d_gates, d_ups, d_n2_parts, down_parts = results
    grad_down = weight_grad(d_down_pieces, acts, lanes)
    grad_gate = weight_grad(normed2_pieces, d_gates, lanes)
    grad_up = weight_grad(normed2_pieces, d_ups, lanes)
    moves = scatter_steps(d_n2_parts, lanes)
    far, _ = next(moves)
    far, grad_down = tie(far, grad_down)
    near, _ = moves.send(far)
    near, (grad_gate, grad_up) = tie(near, (grad_gate, grad_up))
    d_n2 = finish(moves, near)
    (down_parts, grad_down), d_n2 = tie((down_parts, grad_down), d_n2)
    down_moves = scatter_steps(down_parts, lanes)
    down_far, _ = next(down_moves)
    grad_moves = exchange_steps(grad_down.reshape(lanes, out_part, hidden_part), lanes)
    grad_near, _ = next(grad_moves)
    pair_grads = jnp.concatenate(
        [
            grad_gate.reshape(fsdp_size, rows_each, hidden_part),
            grad_up.reshape(fsdp_size, rows_each, hidden_part),
        ],
        1,
    )

    scaled_two = d_n2 * gain_two
    dh = grad_out + inv_two * (
        scaled_two - unit_two * jnp.mean(scaled_two * unit_two, -1, keepdims=True)
    )
    grad_gain_two = jnp.sum(d_n2 * unit_two, 0)
    d_proj = (valid_col * dh).astype(jnp.bfloat16)
    pair_sums = lax.psum_scatter(
        pair_grads, "fsdp", scatter_dimension=0, tiled=False
    ).astype(jnp.float32)
    grad_w_gate = pair_sums[:rows_each]
    grad_w_up = pair_sums[rows_each:]
    out_grad = lax.psum_scatter(
        dot_tn(d_proj, heads_out).astype(jnp.bfloat16).reshape(lanes, out_part, -1),
        "dp",
        scatter_dimension=0,
        tiled=False,
    )
    head_gradient = dot_nn(d_proj, wo_t).astype(jnp.bfloat16)
    d_q_pre, d_kv = attend_back(
        meta,
        low[None],
        high[None],
        query_rows,
        packed_kv,
        head_gradient,
        attention,
        log_total,
        cosine,
        sine,
    )
    (grad_near, down_far), d_q_pre = tie((grad_near, down_far), d_q_pre)
    grad_down = finish(grad_moves, grad_near)
    down_near, _ = down_moves.send(down_far)
    own_kv = scatter_earlier(d_kv, fsdp_size)
    down_near, own_kv = tie(down_near, own_kv)
    down = finish(down_moves, down_near)
    mixed = (hidden + valid_col * down).astype(jnp.bfloat16)
    grad_w_down = (
        lax.psum_scatter(
            grad_down.reshape(fsdp_size, rows_each, hidden_part),
            "fsdp",
            scatter_dimension=0,
            tiled=False,
        )
        .astype(jnp.float32)
        .reshape(pieces_each, out_part, hidden_part)
        .transpose(0, 2, 1)
        .reshape(-1, out_part)
    )
    d_k_pre = rotary_reverse(own_kv[:key_width], cosine, sine).astype(jnp.bfloat16)
    d_v_pre = own_kv[key_width:].astype(jnp.bfloat16)
    d_joint = jnp.concatenate([d_q_pre, d_k_pre, d_v_pre])
    d_n1 = dot_tn(d_joint, joint_t)
    scaled_one = d_n1 * gain_one
    d_tokens = (
        dh + inv_one * (scaled_one - unit_one * jnp.mean(scaled_one * unit_one, -1, keepdims=True))
    ).astype(jnp.bfloat16)
    local_vectors = (
        jnp.sum(d_n1 * unit_one, 0),
        jnp.sum(d_q_pre.astype(jnp.float32), 1),
        jnp.sum(d_v_pre.astype(jnp.float32), 1),
        grad_gain_two,
    )
    vector_rows = jnp.concatenate([v.reshape(lanes, -1) for v in local_vectors], 1)
    vector_rows = jnp.pad(vector_rows, ((0, 0), (0, width - vector_count)))
    vector_rows = jnp.pad(vector_rows[:, None].astype(jnp.bfloat16), ((0, 0), (0, 15), (0, 0)))
    joint_grads = dot_nn(d_joint, normed).astype(jnp.bfloat16)
    joint_parts = jnp.concatenate(
        [
            joint_grads[:query_width].reshape(lanes, query_part, width),
            joint_grads[query_width : query_width + key_width].reshape(lanes, key_part, width),
            joint_grads[query_width + key_width :].reshape(lanes, key_part, width),
            vector_rows,
        ],
        1,
    )
    joint_sum = run(scatter_steps([joint_parts[e] for e in range(lanes)], lanes, ordered=True))
    qkv_rows = query_part + 2 * key_part
    row_sums = scatter_rows(
        jnp.concatenate([joint_sum[:qkv_rows].astype(jnp.bfloat16), out_grad])
        .T.reshape(fsdp_size, rows_each, joint_rows),
        fsdp_size,
    )
    grad_w_query, grad_w_key, grad_w_value, out_grad = [
        row_sums[:, edges[i] : edges[i + 1]] for i in range(4)
    ]
    own_vectors = joint_sum[qkv_rows, :vector_count]
    vector_sum = own_vectors
    for k in range(1, fsdp_size):
        vector_sum = vector_sum + lax.ppermute(
            own_vectors, "fsdp", [(i, (i + k) % fsdp_size) for i in range(fsdp_size)]
        )
    vector_pieces = [vector_sum[marks[i] : marks[i + 1]] for i in range(4)]
    return (
        mixed[None],
        d_tokens[None],
        vector_pieces[0],
        grad_w_query,
        vector_pieces[1],
        grad_w_key,
        grad_w_value,
        vector_pieces[2],
        out_grad,
        vector_pieces[3],
        grad_w_gate,
        grad_w_up,
        grad_w_down,
    )


def solution(mesh):
    placed = (
        P("dp", "fsdp", None),
        P("dp", "fsdp", None),
        P("dp", None),
        P("dp", None),
        P("dp"),
        P("fsdp", "dp"),
        P("dp"),
        P("fsdp", "dp"),
        P("fsdp", "dp"),
        P("dp"),
        P("fsdp", "dp"),
        P("dp"),
        P("fsdp", "dp"),
        P("fsdp", "dp"),
        P("fsdp", "dp"),
    )
    return jax.shard_map(
        body,
        mesh=mesh,
        in_specs=placed,
        out_specs=(
            P("dp", "fsdp", None),
            P("dp", "fsdp", None),
            P("dp"),
            P("fsdp", "dp"),
            P("dp"),
            P("fsdp", "dp"),
            P("fsdp", "dp"),
            P("dp"),
            P("fsdp", "dp"),
            P("dp"),
            P("fsdp", "dp"),
            P("fsdp", "dp"),
            P("fsdp", "dp"),
        ),
        check_vma=False,
    )
```
